32 devices in a mesh: tok: 8 (over z, core), wid: 4 (over y, x).
Axes of the slice: x: 2, y: 2, z: 4, core: 2. Of those that a mesh axis runs over, the one named last changes fastest.
Arguments:
- hidden: bfloat16 [4224, 1280], P('tok', 'wid'), may hold values from -30 to 30
- w_qkv: bfloat16 [1280, 1920], P('tok', 'wid'), may hold values from -0.15625 to 0.15625
- w_out: bfloat16 [1280, 1280], P('tok', 'wid'), may hold values from -0.15625 to 0.15625
- w_gate: bfloat16 [1280, 3584], P('tok', 'wid'), may hold values from -0.15625 to 0.15625
- w_up: bfloat16 [1280, 3584], P('tok', 'wid'), may hold values from -0.15625 to 0.15625
- w_down: bfloat16 [3584, 1280], P('wid', 'tok'), may hold values from -0.125 to 0.125
- g_attn: float32 [1280], replicated, may hold values from 0.1 to 1.9
- g_ffn: float32 [1280], replicated, may hold values from 0.1 to 1.9
- lengths: int32 [136], P('tok'), may hold values from 0 to 2048, as said below
- k_cache: bfloat16 [136, 2048, 320], P('tok', 'wid'), may hold values from -45 to 45
- v_cache: bfloat16 [136, 2048, 320], P('tok', 'wid'), may hold values from -4 to 4
Outputs:
- output: bfloat16 [4224, 1280], P('tok', 'wid')
- new_kv: bfloat16 [4224, 640], P('tok', 'wid')
The draws below stay inside these ranges and needn't reach their ends.
Inputs may be any that keep to these rules, and one draw needn't show every extreme that they name: `lengths`: each request's entry is at most 2048, and some request has exactly 2048.
All inputs are finite; a program needn't handle non-finite values.
Results may differ from the reference program's by a relative error of at most 0.017.
Values may be sent and summed in bfloat16 or wider, within the bound.
A program may use at most 128 MiB of HBM per device.

```python
import jax
import jax.numpy as jnp
from jax import lax

D = 1280
HEADS = 20
KV_HEADS = 5
HEAD_DIM = 64
FF = 3584
STRETCH = 512
MAXLEN = 2048
ROWS_T = 528
REQ_T = 17
ROWS = 4224
REQS = 136
QKVW = 1920
KVW = 320
N_TOK = 8


def draw_hidden(key, part):
    first, second, third = jax.random.split(jax.random.fold_in(key, 11), 3)
    base = jnp.clip(jax.random.normal(first, (ROWS, D), jnp.float32), -4.0, 4.0)
    row_scale = jnp.exp(jax.random.uniform(second, (ROWS, 1), jnp.float32, -1.15, 1.15))
    column_scale = jnp.exp(jax.random.uniform(third, (1, D), jnp.float32, -0.7, 0.7))
    return (base * row_scale * column_scale).astype(jnp.bfloat16)


def draw_lengths(key, part):
    first, second, third = jax.random.split(jax.random.fold_in(key, 23), 3)
    one_draw = jax.random.randint(first, (REQS,), 0, MAXLEN + 1)
    other_draw = jax.random.randint(second, (REQS,), 0, MAXLEN + 1)
    chosen = jax.random.randint(third, (), 0, REQS)
    return jnp.minimum(one_draw, other_draw).at[chosen].set(MAXLEN).astype(jnp.int32)


def draw_k_cache(key, part):
    first = jax.random.fold_in(jax.random.fold_in(key, 37), 0)
    base = jnp.clip(jax.random.normal(first, (REQS, MAXLEN, KVW), jnp.float32), -4.0, 4.0)
    return base.astype(jnp.bfloat16)


def raised(drawn, stream_key, source, target, shards_of, factor):
    def block_of(axis_at):
        return (jnp.arange(drawn.shape[axis_at]) // (drawn.shape[axis_at] // shards_of)).reshape((-1,) + (1,) * (drawn.ndim - 1 - axis_at))

    near = jax.random.permutation(stream_key, shards_of)[block_of(target)]
    other_side = (block_of(target) + shards_of // 2) % shards_of
    return jnp.where((block_of(source) == near) | (block_of(source) == other_side), factor * drawn, drawn)


def shard_levels(own_key, shape, pieces, least, high):
    def one(dim, blocks):
        draws = jax.random.uniform(jax.random.fold_in(jax.random.fold_in(own_key, 6), dim), (blocks,), jnp.float32, least / len(pieces), high / len(pieces))
        return jnp.repeat(jnp.exp(draws), shape[dim] // blocks).reshape((-1,) + (1,) * (len(shape) - dim - 1))

    level = one(*pieces[0])
    for cut in pieces[1:]:
        level = level * one(*cut)
    return level


def normal_values(key, extent, scale, bound, pieces=(), kind=jnp.bfloat16):
    entries = scale * jax.random.normal(key, extent, jnp.float32)
    if pieces:
        entries = entries * shard_levels(key, extent, pieces, -0.22, 0.18)
    return jnp.clip(entries, -bound, bound).astype(kind)


def gaussian_with(rng, extent, spread, most, cuts, heavy, kind=jnp.bfloat16):
    values = spread * jax.random.normal(rng, extent, jnp.float32)
    if cuts:
        values = values * shard_levels(rng, extent, cuts, -0.22, 0.18)
    return jnp.clip(raised(values, jax.random.fold_in(rng, 3), *heavy), -most, most).astype(kind)


def setup_inputs(seed: int = 0) -> dict:
    seeds = jax.random.split(jax.random.key(seed), 12)
    return {
        "hidden": draw_hidden(jax.random.fold_in(seeds[11], 71), 0),
        "w_qkv": normal_values(seeds[1], (D, QKVW), D ** -0.5, 0.15625, ((0, 8), (1, 4))),
        "w_out": normal_values(seeds[2], (HEADS * HEAD_DIM, D), (HEADS * HEAD_DIM) ** -0.5, 0.15625, ((0, 8), (1, 4))),
        "w_gate": normal_values(seeds[3], (D, FF), D ** -0.5, 0.15625, ((0, 8), (1, 4))),
        "w_up": normal_values(seeds[4], (D, FF), D ** -0.5, 0.15625, ((0, 8), (1, 4))),
        "w_down": gaussian_with(seeds[5], (FF, D), FF ** -0.5, 0.125, ((0, 4), (1, 8)), (0, 1, 8, 2.0)),
        "g_attn": jnp.clip(1.0 + 0.18 * jax.random.normal(seeds[6], (D,), jnp.float32), 0.1, 1.9),
        "g_ffn": jnp.clip(1.0 + 0.18 * jax.random.normal(seeds[7], (D,), jnp.float32), 0.1, 1.9),
        "lengths": draw_lengths(jax.random.fold_in(seeds[11], 71), 0),
        "k_cache": draw_k_cache(jax.random.fold_in(seeds[11], 71), 0),
        "v_cache": normal_values(seeds[10], (REQS, MAXLEN, KVW), 1.0, 4.0, ((0, 8), (1, 4))),
    }


EPSILON = 1e-05
MASKED = -1e+30
SCORE_SCALE = 0.125

def settle(values):
    return lax.optimization_barrier(values.astype(jnp.bfloat16))

def norm_rows(values, gain):
    wide = values.astype(jnp.float32)
    mean_square = lax.optimization_barrier(jnp.mean(wide * wide, axis=-1, keepdims=True))
    return (wide * lax.rsqrt(mean_square + EPSILON) * gain).astype(jnp.bfloat16)

def rotate(parts, places):
    half = parts.shape[-1] // 2
    ladder = jnp.arange(half).astype(jnp.float32) * (2.0 / parts.shape[-1])
    freqs = jnp.power(10000.0, -ladder)
    angles = places.astype(jnp.float32)[:, None] * freqs[None, :]
    cosine = jnp.cos(angles)[:, None, :]
    sine = jnp.sin(angles)[:, None, :]
    first = parts[..., :half]
    second = parts[..., half:]
    return jnp.concatenate([first * cosine - second * sine, second * cosine + first * sine], axis=-1)

def positions(owned):
    stretch_rows = owned[0] + jnp.arange(STRETCH).astype(jnp.int32)
    return jnp.concatenate([stretch_rows, owned[1:]])

def attend(inputs):
    query, keys, values, k_old, v_old, owned = inputs
    groups = HEADS // KV_HEADS
    query_heads = query.reshape(ROWS_T, KV_HEADS, groups, HEAD_DIM).astype(jnp.float32)
    old_keys = k_old.reshape(REQ_T, MAXLEN, KV_HEADS, HEAD_DIM).astype(jnp.float32)
    old_values = v_old.reshape(REQ_T, MAXLEN, KV_HEADS, HEAD_DIM).astype(jnp.float32)
    spots = jnp.arange(MAXLEN).astype(jnp.int32)
    live = spots[None, :] < owned[:, None]
    score_stretch = jnp.einsum('rkgd,pkd->rkgp', query_heads[:STRETCH], old_keys[0]) * SCORE_SCALE
    score_stretch = jnp.where(live[0][None, None, None, :], score_stretch, MASKED)
    score_decode = jnp.einsum('jkgd,jpkd->jkgp', query_heads[STRETCH:], old_keys[1:]) * SCORE_SCALE
    score_decode = jnp.where(live[1:][:, None, None, :], score_decode, MASKED)
    row_ids = jnp.arange(ROWS_T).astype(jnp.int32)
    later = row_ids[:, None]
    earlier = row_ids[None, :]
    fresh_ok = (later < STRETCH) & (earlier < STRETCH) & (earlier <= later) | (later >= STRETCH) & (earlier == later)
    score_fresh = jnp.einsum('rkgd,jkd->rkgj', query_heads, keys.astype(jnp.float32)) * SCORE_SCALE
    score_fresh = jnp.where(fresh_ok[:, None, None, :], score_fresh, MASKED)
    peak = jnp.maximum(jnp.concatenate([score_stretch.max(-1), score_decode.max(-1)], axis=0), score_fresh.max(-1))
    expo_stretch = jnp.exp(score_stretch - peak[:STRETCH, :, :, None])
    expo_decode = jnp.exp(score_decode - peak[STRETCH:, :, :, None])
    expo_fresh = jnp.exp(score_fresh - peak[:, :, :, None])
    totals = jnp.concatenate([expo_stretch.sum(-1), expo_decode.sum(-1)], axis=0) + expo_fresh.sum(-1)
    cached = jnp.concatenate([jnp.einsum('rkgp,pkd->rkgd', settle(expo_stretch).astype(jnp.float32), old_values[0]), jnp.einsum('jkgp,jpkd->jkgd', settle(expo_decode).astype(jnp.float32), old_values[1:])], axis=0)
    fresh = jnp.einsum('rkgj,jkd->rkgd', settle(expo_fresh).astype(jnp.float32), values.astype(jnp.float32))
    result = (cached + fresh) / totals[:, :, :, None]
    return result.astype(jnp.bfloat16).reshape(ROWS_T, HEADS * HEAD_DIM)

def reference(hidden, w_qkv, w_out, w_gate, w_up, w_down, g_attn, g_ffn, lengths, k_cache, v_cache):
    query_width = HEADS * HEAD_DIM
    normed = norm_rows(hidden, g_attn)
    mixed = settle(jnp.dot(normed, w_qkv, preferred_element_type=jnp.float32))
    owned = lengths.reshape(N_TOK, REQ_T)
    places = jax.vmap(positions)(owned).reshape(ROWS)
    query = rotate(mixed[:, :query_width].astype(jnp.float32).reshape(ROWS, HEADS, HEAD_DIM), places).astype(jnp.bfloat16)
    keys = rotate(mixed[:, query_width:query_width + KVW].astype(jnp.float32).reshape(ROWS, KV_HEADS, HEAD_DIM), places).astype(jnp.bfloat16)
    values = mixed[:, query_width + KVW:]
    new_kv = jnp.concatenate([keys.reshape(ROWS, KVW), values], axis=1)
    attended = lax.map(attend, (query.reshape(N_TOK, ROWS_T, HEADS, HEAD_DIM), keys.reshape(N_TOK, ROWS_T, KV_HEADS, HEAD_DIM), values.reshape(N_TOK, ROWS_T, KV_HEADS, HEAD_DIM), k_cache.reshape(N_TOK, REQ_T, MAXLEN, KVW), v_cache.reshape(N_TOK, REQ_T, MAXLEN, KVW), owned)).reshape(ROWS, query_width)
    residual = hidden.astype(jnp.float32) + jnp.dot(attended, w_out, preferred_element_type=jnp.float32)
    middle = settle(residual)
    normed_ffn = norm_rows(middle, g_ffn)
    gate = jnp.dot(normed_ffn, w_gate, preferred_element_type=jnp.float32)
    up = jnp.dot(normed_ffn, w_up, preferred_element_type=jnp.float32)
    activated = (jax.nn.silu(gate) * up).astype(jnp.bfloat16)
    output = (residual + jnp.dot(activated, w_down, preferred_element_type=jnp.float32)).astype(jnp.bfloat16)
    return (output, new_kv)
```

```python
import functools

import jax
import jax.numpy as jnp
from jax import lax
from jax.experimental import pallas as pl
from jax.experimental.pallas import tpu as pltpu
from jax.sharding import PartitionSpec as P

HEADS = 20
KV_HEADS = 5
HEAD_DIM = 64
STRETCH = 512


EPSILON = 1e-05
MASKED = -1e30
SCORE_SCALE = 0.125


def norm_rows(values, gain):
    wide = values.astype(jnp.float32)
    mean_square = jnp.mean(wide * wide, axis=-1, keepdims=True)
    return (wide * lax.rsqrt(mean_square + EPSILON) * gain).astype(jnp.bfloat16)


def rotate(parts, places):
    half = parts.shape[-1] // 2
    ladder = jnp.arange(half).astype(jnp.float32) * (2.0 / parts.shape[-1])
    freqs = jnp.power(10000.0, -ladder)
    angles = places.astype(jnp.float32)[:, None] * freqs[None, :]
    cosine = jnp.cos(angles)[:, None, :]
    sine = jnp.sin(angles)[:, None, :]
    first = parts[..., :half]
    second = parts[..., half:]
    return jnp.concatenate(
        [first * cosine - second * sine, second * cosine + first * sine], axis=-1
    )


def shards_plain(hidden, w_qkv, w_out, w_gate, w_up, w_down, g_attn, g_ffn, lengths, k_cache, v_cache):
    wid_count = lax.axis_size("wid")
    wid_place = lax.axis_index("wid")
    row_count = hidden.shape[0]
    query_width = HEADS * HEAD_DIM
    kv_width = KV_HEADS * HEAD_DIM
    groups = HEADS // KV_HEADS
    full_rows = lax.all_gather(hidden, "wid", axis=1, tiled=True)
    normed = norm_rows(full_rows, g_attn)
    tall_cols = lax.all_gather(w_qkv, "tok", axis=0, tiled=True)
    own_cols = jnp.dot(normed, tall_cols, preferred_element_type=jnp.float32)
    mixed = lax.all_gather(own_cols.astype(jnp.bfloat16), "wid", axis=1, tiled=True)
    stretch_rows = lengths[0] + jnp.arange(STRETCH)
    places = jnp.concatenate([stretch_rows, lengths[1:]])
    query = rotate(
        mixed[:, :query_width].astype(jnp.float32).reshape(row_count, HEADS, HEAD_DIM), places
    ).astype(jnp.bfloat16)
    keys = rotate(
        mixed[:, query_width : query_width + kv_width]
        .astype(jnp.float32)
        .reshape(row_count, KV_HEADS, HEAD_DIM),
        places,
    ).astype(jnp.bfloat16)
    values = mixed[:, query_width + kv_width :]
    new_kv_all = jnp.concatenate([keys.reshape(row_count, kv_width), values], axis=1)
    kv_share = 2 * kv_width // wid_count
    new_kv = lax.dynamic_slice_in_dim(new_kv_all, wid_place * kv_share, kv_share, 1)
    value_heads = values.reshape(row_count, KV_HEADS, HEAD_DIM)
    span = k_cache.shape[1]
    requests = k_cache.shape[0]
    query_heads = query.reshape(row_count, KV_HEADS, groups, HEAD_DIM)
    old_keys = k_cache.reshape(requests, span, KV_HEADS, HEAD_DIM)
    old_values = v_cache.reshape(requests, span, KV_HEADS, HEAD_DIM)
    spots = wid_place * span + jnp.arange(span)
    live = spots[None, :] < lengths[:, None]
    score_stretch = (
        jnp.einsum(
            "rkgd,pkd->rkgp", query_heads[:STRETCH], old_keys[0], preferred_element_type=jnp.float32
        )
        * SCORE_SCALE
    )
    score_stretch = jnp.where(live[0][None, None, None, :], score_stretch, MASKED)
    score_decode = (
        jnp.einsum(
            "jkgd,jpkd->jkgp",
            query_heads[STRETCH:],
            old_keys[1:],
            preferred_element_type=jnp.float32,
        )
        * SCORE_SCALE
    )
    score_decode = jnp.where(live[1:][:, None, None, :], score_decode, MASKED)
    band = row_count // wid_count
    first_row = wid_place * band
    query_mine = lax.dynamic_slice_in_dim(query_heads, first_row, band, 0)
    later = first_row + jnp.arange(band)[:, None]
    earlier = jnp.arange(row_count)[None, :]
    fresh_ok = (later < STRETCH) & (earlier < STRETCH) & (earlier <= later) | (later >= STRETCH) & (
        earlier == later
    )
    score_fresh = (
        jnp.einsum("rkgd,jkd->rkgj", query_mine, keys, preferred_element_type=jnp.float32)
        * SCORE_SCALE
    )
    score_fresh = jnp.where(fresh_ok[:, None, None, :], score_fresh, MASKED)
    cache_peak = jnp.concatenate([score_stretch.max(-1), score_decode.max(-1)], axis=0)
    fresh_peak = lax.dynamic_update_slice_in_dim(
        jnp.full(cache_peak.shape, MASKED, jnp.float32), score_fresh.max(-1), first_row, 0
    )
    peak = lax.pmax(jnp.maximum(cache_peak, fresh_peak).astype(jnp.bfloat16), "wid").astype(
        jnp.float32
    )
    expo_stretch = jnp.exp(score_stretch - peak[:STRETCH, :, :, None])
    expo_decode = jnp.exp(score_decode - peak[STRETCH:, :, :, None])
    peak_mine = lax.dynamic_slice_in_dim(peak, first_row, band, 0)
    expo_fresh = jnp.exp(score_fresh - peak_mine[:, :, :, None])
    totals = jnp.concatenate([expo_stretch.sum(-1), expo_decode.sum(-1)], axis=0)
    sums = jnp.concatenate(
        [
            jnp.einsum(
                "rkgp,pkd->rkgd",
                expo_stretch.astype(jnp.bfloat16),
                old_values[0],
                preferred_element_type=jnp.float32,
            ),
            jnp.einsum(
                "jkgp,jpkd->jkgd",
                expo_decode.astype(jnp.bfloat16),
                old_values[1:],
                preferred_element_type=jnp.float32,
            ),
        ],
        axis=0,
    )
    fresh_sums = jnp.einsum(
        "rkgj,jkd->rkgd",
        expo_fresh.astype(jnp.bfloat16),
        value_heads,
        preferred_element_type=jnp.float32,
    )
    sums = lax.dynamic_update_slice_in_dim(
        sums, lax.dynamic_slice_in_dim(sums, first_row, band, 0) + fresh_sums, first_row, 0
    )
    totals = lax.dynamic_update_slice_in_dim(
        totals,
        lax.dynamic_slice_in_dim(totals, first_row, band, 0) + expo_fresh.sum(-1),
        first_row,
        0,
    )
    sums_all, totals_all = (
        lax.psum(sums.reshape(row_count, query_width).astype(jnp.bfloat16), "wid").astype(
            jnp.float32
        ),
        lax.psum(totals.reshape(row_count, HEADS).astype(jnp.bfloat16), "wid").astype(jnp.float32),
    )
    merged = sums_all.reshape(row_count, HEADS, HEAD_DIM) / totals_all[:, :, None]
    attended = merged.astype(jnp.bfloat16).reshape(row_count, query_width)
    out_whole = lax.all_gather(w_out, "tok", axis=0, tiled=True)
    projected = jnp.dot(attended, out_whole, preferred_element_type=jnp.float32)
    residual = hidden.astype(jnp.float32) + projected
    middle = residual.astype(jnp.bfloat16)
    middle_full = lax.all_gather(middle, "wid", axis=1, tiled=True)
    normed_ffn = norm_rows(middle_full, g_ffn)
    gate_whole, up_whole = (
        lax.all_gather(w_gate, "tok", axis=0, tiled=True),
        lax.all_gather(w_up, "tok", axis=0, tiled=True),
    )
    gate = jnp.dot(normed_ffn, gate_whole, preferred_element_type=jnp.float32)
    up = jnp.dot(normed_ffn, up_whole, preferred_element_type=jnp.float32)
    activated = (jax.nn.silu(gate) * up).astype(jnp.bfloat16)
    down_full = lax.all_gather(w_down, "tok", axis=1, tiled=True)
    own_sums = lax.psum_scatter(
        lax.dot_general(
            down_full, activated, (((0,), (1,)), ((), ())), preferred_element_type=jnp.float32
        ).astype(jnp.bfloat16),
        "wid",
        scatter_dimension=0,
        tiled=True,
    ).astype(jnp.float32)
    output = (residual + own_sums.T).astype(jnp.bfloat16)
    return (output, new_kv)


MESH = pl.DeviceIdType.MESH
VMEM_LIMIT = 56 * 1024 * 1024


def vmem():
    return pl.BlockSpec(memory_space=pltpu.VMEM)


def params(ident):
    return pltpu.CompilerParams(
        collective_id=ident, has_side_effects=True, vmem_limit_bytes=VMEM_LIMIT
    )


def greet(peers):
    barrier = pltpu.get_barrier_semaphore()
    for peer in peers:
        pl.semaphore_signal(barrier, inc=1, device_id=peer, device_id_type=MESH)
    pl.semaphore_wait(barrier, len(peers))


def push(src, dst, send, recv, peer):
    copy = pltpu.make_async_remote_copy(
        src_ref=src,
        dst_ref=dst,
        send_sem=send,
        recv_sem=recv,
        device_id=peer,
        device_id_type=MESH,
    )
    copy.start()
    return copy


def wid_peers(count):
    tok_place = lax.axis_index("tok")
    wid_place = lax.axis_index("wid")
    return [(tok_place, lax.rem(wid_place + k, count)) for k in range(1, count)]


def share(src, slots, send, recv, peers, place):
    return [push(src, slots.at[place], send.at[k], recv.at[k], peer) for k, peer in enumerate(peers)]


def mix_kernel(
    wids, toks, hidden, weight, gain, cosine, sine, turn, out,
    rows_all, weight_all, mixed_all, wide, send_a, recv_a, send_b, recv_b, send_c, recv_c, send_d, recv_d,
):
    wid_place = lax.axis_index("wid")
    tok_place = lax.axis_index("tok")
    chips = toks // 2
    chip = tok_place // 2
    core = lax.rem(tok_place, 2)
    peers = wid_peers(wids)
    line = [(2 * lax.rem(chip + k, chips) + core, wid_place) for k in range(1, chips)]
    twin = (2 * chip + 1 - core, wid_place)
    greet(peers + line + [twin])
    row_copies = share(hidden, rows_all, send_a, recv_a, peers, wid_place)
    line_copies = share(weight, weight_all, send_b, recv_b, line, tok_place)
    twin_copies = [push(weight, weight_all.at[tok_place], send_c.at[0], recv_c.at[0], twin)]
    rows_all[wid_place] = hidden[...]
    weight_all[tok_place] = weight[...]
    for k, copy in enumerate(line_copies):
        copy.wait_recv()
        source = 2 * lax.rem(chip + chips - k - 1, chips) + core
        slot = weight_all.at[source]
        twin_copies.append(push(slot, slot, send_c.at[k + 1], recv_c.at[k + 1], twin))
    for copy in row_copies:
        copy.wait_recv()
    square = 0.0
    for w in range(wids):
        part = rows_all[w].astype(jnp.float32)
        square = square + jnp.sum(part * part, axis=-1, keepdims=True)
    scale = lax.rsqrt(square * (1.0 / (wids * hidden.shape[1])) + EPSILON)
    for copy in twin_copies:
        copy.wait_recv()
    per = toks // wids
    total = None
    for w in range(wids):
        normed = (rows_all[w].astype(jnp.float32) * scale * gain[w]).astype(jnp.bfloat16)
        block = weight_all[per * w : per * (w + 1)].reshape(hidden.shape[1], weight.shape[1])
        term = jnp.dot(normed, block, preferred_element_type=jnp.float32)
        total = term if total is None else total + term
    mixed_all[wid_place] = total.astype(jnp.bfloat16)
    mixed_copies = share(mixed_all.at[wid_place], mixed_all, send_d, recv_d, peers, wid_place)
    for copy in mixed_copies:
        copy.wait_recv()
    width = weight.shape[1]
    for w in range(wids):
        wide[:, w * width : (w + 1) * width] = mixed_all[w].astype(jnp.float32)
    turned = (HEADS + KV_HEADS) * HEAD_DIM
    for start in range(0, wids * width, 128):
        part = wide[:, start : start + 128]
        if start < turned:
            swapped = jnp.dot(
                part.astype(jnp.bfloat16), turn[...], preferred_element_type=jnp.float32
            )
            spun = part * cosine[...] + swapped * sine[...]
            if start + 128 > turned:
                lane = lax.broadcasted_iota(jnp.int32, spun.shape, 1)
                spun = jnp.where(lane < turned - start, spun, part)
            part = spun
        out[:, start : start + 128] = part.astype(jnp.bfloat16)
    for copy in row_copies + line_copies + twin_copies + mixed_copies:
        copy.wait_send()


def mix(wids, toks, hidden, w_qkv, gain, cosine, sine, turn):
    rows, width = hidden.shape
    depth, columns = w_qkv.shape
    dma = pltpu.SemaphoreType.DMA
    chips = toks // 2
    return pl.pallas_call(
        functools.partial(mix_kernel, wids, toks),
        out_shape=jax.ShapeDtypeStruct((rows, wids * columns), jnp.bfloat16),
        in_specs=[vmem()] * 6,
        out_specs=vmem(),
        scratch_shapes=[
            pltpu.VMEM((wids, rows, width), jnp.bfloat16),
            pltpu.VMEM((toks, depth, columns), jnp.bfloat16),
            pltpu.VMEM((wids, rows, columns), jnp.bfloat16),
            pltpu.VMEM((rows, wids * columns), jnp.float32),
            dma((wids - 1,)), dma((wids - 1,)),
            dma((chips - 1,)), dma((chips - 1,)),
            dma((chips,)), dma((chips,)),
            dma((wids - 1,)), dma((wids - 1,)),
        ],
        compiler_params=params(0),
        cost_estimate=pl.CostEstimate(flops=10**10, bytes_accessed=10**8, transcendentals=0),
    )(hidden, w_qkv, gain, cosine, sine, turn)


def partial_kernel(wids, lengths, mixed, spread, k_old, v_old, sums, stats, dec_sums, dec_stats):
    place = lax.axis_index("wid")
    span = k_old.shape[1]
    fresh = STRETCH // wids
    query_width = HEADS * HEAD_DIM
    kv_width = KV_HEADS * HEAD_DIM
    per = HEADS // wids
    groups = HEADS // KV_HEADS
    base = place * span
    first = pl.multiple_of(place * fresh, fresh)
    row = lax.broadcasted_iota(jnp.int32, (STRETCH, span + fresh), 0)
    spot = lax.broadcasted_iota(jnp.int32, (STRETCH, span + fresh), 1)
    limit = lengths[0] - base
    seen = ((spot < span) & (spot < limit)) | ((spot >= span) & (spot - span + first <= row))
    bias = jnp.where(seen, 0.0, MASKED)
    for g in range(KV_HEADS):
        at = g * HEAD_DIM
        keys = jnp.concatenate(
            [
                k_old[0, :, at : at + HEAD_DIM],
                mixed[pl.ds(first, fresh), query_width + at : query_width + at + HEAD_DIM],
            ],
            axis=0,
        )
        held = query_width + kv_width + at
        values = jnp.concatenate(
            [v_old[0, :, at : at + HEAD_DIM], mixed[pl.ds(first, fresh), held : held + HEAD_DIM]],
            axis=0,
        )
        for h in range(g * groups, (g + 1) * groups):
            query = mixed[:STRETCH, h * HEAD_DIM : (h + 1) * HEAD_DIM] * jnp.bfloat16(SCORE_SCALE)
            score = (
                lax.dot_general(
                    query, keys, (((1,), (1,)), ((), ())), preferred_element_type=jnp.float32
                )
                + bias
            )
            peak = jnp.max(score, axis=1, keepdims=True)
            expo = jnp.exp(score - peak)
            total = jnp.sum(expo, axis=1, keepdims=True)
            part = jnp.dot(expo.astype(jnp.bfloat16), values, preferred_element_type=jnp.float32)
            d, i = h // per, h % per
            sums[d, :, i * HEAD_DIM : (i + 1) * HEAD_DIM] = part.astype(jnp.bfloat16)
            stats[d, :, i : i + 1] = peak
            stats[d, :, per + i : per + i + 1] = total
    rows = spread.shape[1]
    spots = lax.broadcasted_iota(jnp.int32, (rows, span), 1) + base

    def one(j, carry):
        query = spread[j]
        score = (
            lax.dot_general(
                query, k_old[j + 1], (((1,), (1,)), ((), ())), preferred_element_type=jnp.float32
            )
            * SCORE_SCALE
        )
        score = jnp.where(spots < lengths[j + 1], score, MASKED)
        line = mixed[pl.ds(STRETCH, 16), query_width:].astype(jnp.float32)
        pick = lax.broadcasted_iota(jnp.int32, line.shape, 0) == j
        line = jnp.sum(jnp.where(pick, line, 0.0), axis=0, keepdims=True)
        own = (
            jnp.sum(query.astype(jnp.float32) * line[:, :kv_width], axis=1, keepdims=True)
            * SCORE_SCALE
        )
        own = jnp.where(place == 0, own, MASKED)
        peak = jnp.maximum(jnp.max(score, axis=1, keepdims=True), own)
        expo = jnp.exp(score - peak)
        expo_own = jnp.exp(own - peak)
        expo_own = jnp.where(place == 0, expo_own, 0.0)
        total = jnp.sum(expo, axis=1, keepdims=True) + expo_own
        part = jnp.dot(
            expo.astype(jnp.bfloat16), v_old[j + 1], preferred_element_type=jnp.float32
        )
        dec_sums[j] = part + expo_own * line[:, kv_width:]
        dec_stats[j, :, 0:1] = peak
        dec_stats[j, :, 1:2] = total
        return carry

    lax.fori_loop(0, k_old.shape[0] - 1, one, 0)


def partials(wids, lengths, mixed, spread, k_cache, v_cache):
    per = HEADS // wids
    count, rows, width = spread.shape
    return pl.pallas_call(
        functools.partial(partial_kernel, wids),
        out_shape=(
            jax.ShapeDtypeStruct((wids, STRETCH, per * HEAD_DIM), jnp.bfloat16),
            jax.ShapeDtypeStruct((wids, STRETCH, 2 * per), jnp.float32),
            jax.ShapeDtypeStruct((count, rows, width), jnp.float32),
            jax.ShapeDtypeStruct((count, rows, 2), jnp.float32),
        ),
        in_specs=[pl.BlockSpec(memory_space=pltpu.SMEM)] + [vmem()] * 4,
        out_specs=(vmem(),) * 4,
        compiler_params=pltpu.CompilerParams(vmem_limit_bytes=VMEM_LIMIT),
        cost_estimate=pl.CostEstimate(flops=10**10, bytes_accessed=10**8, transcendentals=10**7),
    )(lengths, mixed, spread, k_cache, v_cache)


def swap_kernel(wids, sums, stats, sums_all, stats_all, send_a, recv_a, send_b, recv_b):
    place = lax.axis_index("wid")
    peers = wid_peers(wids)
    greet(peers)
    copies = []
    for k, peer in enumerate(peers):
        copies.append(push(stats.at[peer[1]], stats_all.at[place], send_b.at[k], recv_b.at[k], peer))
        copies.append(push(sums.at[peer[1]], sums_all.at[place], send_a.at[k], recv_a.at[k], peer))
    stats_all[place] = stats[place]
    sums_all[place] = sums[place]
    for copy in copies:
        copy.wait()


def swap(wids, sums, stats):
    dma = pltpu.SemaphoreType.DMA
    return pl.pallas_call(
        functools.partial(swap_kernel, wids),
        out_shape=(
            jax.ShapeDtypeStruct(sums.shape, sums.dtype),
            jax.ShapeDtypeStruct(stats.shape, stats.dtype),
        ),
        in_specs=[vmem()] * 2,
        out_specs=(vmem(),) * 2,
        scratch_shapes=[dma((wids - 1,))] * 4,
        compiler_params=params(1),
        cost_estimate=pl.CostEstimate(flops=10**10, bytes_accessed=10**8, transcendentals=0),
    )(sums, stats)


def finish_kernel(
    wids, toks, attended, hidden, w_out, w_gate, w_up, w_down, gain, out,
    att_all, mid_all, part_all, part_own, residual, active,
    send_a, recv_a, send_b, recv_b, send_c, recv_c,
):
    place = lax.axis_index("wid")
    peers = wid_peers(wids)
    greet(peers)
    width = hidden.shape[1]
    att_copies = share(attended, att_all, send_a, recv_a, peers, place)
    att_all[place] = attended[...]
    for copy in att_copies:
        copy.wait_recv()
    total = hidden[...].astype(jnp.float32)
    for w in range(wids):
        total = total + jnp.dot(
            att_all[w], w_out[w * width : (w + 1) * width, :], preferred_element_type=jnp.float32
        )
    residual[...] = total
    mid_all[place] = total.astype(jnp.bfloat16)
    mid_copies = share(mid_all.at[place], mid_all, send_b, recv_b, peers, place)
    for copy in mid_copies:
        copy.wait_recv()
    square = 0.0
    for w in range(wids):
        part = mid_all[w].astype(jnp.float32)
        square = square + jnp.sum(part * part, axis=-1, keepdims=True)
    scale = lax.rsqrt(square * (1.0 / (wids * width)) + EPSILON)
    normed = [
        (mid_all[w].astype(jnp.float32) * scale * gain[w]).astype(jnp.bfloat16)
        for w in range(wids)
    ]
    hidden_units = w_gate.shape[1]
    for start in range(0, hidden_units, 128):
        gate = 0.0
        up = 0.0
        for w in range(wids):
            at = slice(w * width, (w + 1) * width)
            gate = gate + jnp.dot(
                normed[w], w_gate[at, start : start + 128], preferred_element_type=jnp.float32
            )
            up = up + jnp.dot(
                normed[w], w_up[at, start : start + 128], preferred_element_type=jnp.float32
            )
        active[:, start : start + 128] = (gate / (1.0 + jnp.exp(-gate)) * up).astype(jnp.bfloat16)
    per = toks // wids
    narrow = w_down.shape[2]
    copies = []
    for k in list(range(1, wids)) + [0]:
        dest = lax.rem(place + k, wids)
        for i in range(per):
            part_own[k, :, i * narrow : (i + 1) * narrow] = jnp.dot(
                active[...], w_down[dest * per + i], preferred_element_type=jnp.float32
            ).astype(jnp.bfloat16)
        if k:
            copies.append(
                push(
                    part_own.at[k], part_all.at[k - 1], send_c.at[k - 1], recv_c.at[k - 1],
                    peers[k - 1],
                )
            )
    total = residual[...] + part_own[0].astype(jnp.float32)
    for k, copy in enumerate(copies):
        copy.wait_recv()
        total = total + part_all[k].astype(jnp.float32)
    out[...] = total.astype(jnp.bfloat16)
    for copy in att_copies + mid_copies + copies:
        copy.wait_send()


def finish(wids, toks, attended, hidden, w_out, w_gate, w_up, w_down, gain):
    rows, width = hidden.shape
    dma = pltpu.SemaphoreType.DMA
    slots = pltpu.VMEM((wids, rows, width), jnp.bfloat16)
    return pl.pallas_call(
        functools.partial(finish_kernel, wids, toks),
        out_shape=jax.ShapeDtypeStruct((rows, width), jnp.bfloat16),
        in_specs=[vmem()] * 7,
        out_specs=vmem(),
        scratch_shapes=[
            slots,
            slots,
            pltpu.VMEM((wids - 1, rows, width), jnp.bfloat16),
            slots,
            pltpu.VMEM((rows, width), jnp.float32),
            pltpu.VMEM((rows, w_gate.shape[1]), jnp.bfloat16),
        ]
        + [dma((wids - 1,))] * 6,
        compiler_params=params(2),
        cost_estimate=pl.CostEstimate(flops=10**10, bytes_accessed=10**8, transcendentals=0),
    )(attended, hidden, w_out, w_gate, w_up, w_down, gain)


def shards_kernels(hidden, w_qkv, w_out, w_gate, w_up, w_down, g_attn, g_ffn, lengths, k_cache, v_cache):
    wids = lax.axis_size("wid")
    toks = lax.axis_size("tok")
    place = lax.axis_index("wid")
    rows, width = hidden.shape
    query_width = HEADS * HEAD_DIM
    kv_width = KV_HEADS * HEAD_DIM
    per = HEADS // wids
    groups = HEADS // KV_HEADS
    out_whole = lax.all_gather(w_out, "tok", axis=0, tiled=True)
    gate_whole = lax.all_gather(w_gate, "tok", axis=0, tiled=True)
    up_whole = lax.all_gather(w_up, "tok", axis=0, tiled=True)
    down_whole = lax.all_gather(w_down, "tok", axis=0, tiled=False)
    places = jnp.concatenate([lengths[0] + jnp.arange(STRETCH), lengths[1:]])
    half = HEAD_DIM // 2
    ladder = jnp.arange(half).astype(jnp.float32) * (2.0 / HEAD_DIM)
    freqs = jnp.power(10000.0, -ladder)
    angles = places.astype(jnp.float32)[:, None] * freqs[None, :]
    cos, sin = jnp.cos(angles), jnp.sin(angles)
    cosine = jnp.concatenate([cos, cos, cos, cos], axis=1)
    sine = jnp.concatenate([-sin, sin, -sin, sin], axis=1)
    lanes = jnp.arange(128)
    turn = (lanes[:, None] == (lanes ^ half)[None, :]).astype(jnp.bfloat16)
    mixed = mix(wids, toks, hidden, w_qkv, g_attn.reshape(wids, 1, width), cosine, sine, turn)
    share_width = 2 * kv_width // wids
    new_kv = lax.dynamic_slice_in_dim(mixed, query_width + place * share_width, share_width, 1)
    count = rows - STRETCH
    own = mixed[STRETCH:, :query_width].reshape(count, HEADS, 1, HEAD_DIM)
    member = (jnp.arange(HEADS) // groups)[:, None] == jnp.arange(KV_HEADS)[None, :]
    spread = jnp.where(member[None, :, :, None], own, jnp.bfloat16(0)).reshape(count, HEADS, kv_width)
    spread = jnp.pad(spread, ((0, 0), (0, 32 - HEADS), (0, 0)))
    sums, stats, dec_sums, dec_stats = partials(wids, lengths, mixed, spread, k_cache, v_cache)
    dec = dec_sums[:, :HEADS].reshape(count, HEADS, KV_HEADS, HEAD_DIM)
    dec = jnp.where(member[None, :, :, None], dec, 0.0).sum(2).astype(jnp.bfloat16)
    dec = dec.reshape(count, wids, per * HEAD_DIM).transpose(1, 0, 2)
    sums = jnp.concatenate([sums, dec], axis=1)
    dec_stats = dec_stats[:, :HEADS].reshape(count, wids, per, 2).transpose(1, 3, 2, 0)
    stats = stats.transpose(0, 2, 1)
    stats = jnp.concatenate([stats, dec_stats.reshape(wids, 2 * per, count)], axis=2)
    stats = jnp.pad(stats, ((0, 0), (0, 16 - 2 * per), (0, 0)))
    sums, stats = swap(wids, sums, stats)
    peaks, totals = stats[:, :per], stats[:, per : 2 * per]
    weight = jnp.exp(peaks - peaks.max(0, keepdims=True))
    weight = weight / (weight * totals).sum(0, keepdims=True)
    weight = jnp.repeat(weight.transpose(0, 2, 1), HEAD_DIM, axis=2)
    attended = (sums.astype(jnp.float32) * weight).sum(0).astype(jnp.bfloat16)
    output = finish(
        wids, toks, attended, hidden, out_whole, gate_whole, up_whole, down_whole,
        g_ffn.reshape(wids, 1, width),
    )
    return (output, new_kv)


def shards(*args):
    wids, toks = lax.axis_size("wid"), lax.axis_size("tok")
    fits = HEADS % wids == 0 and STRETCH % (128 * wids) == 0 and toks % (2 * wids) == 0
    fits = fits and args[1].shape[0] % 16 == 0 and args[3].shape[1] % 128 == 0
    return (shards_kernels if fits else shards_plain)(*args)


def solution(mesh):
    placed = (
        P("tok", "wid"),
        P("tok", "wid"),
        P("tok", "wid"),
        P("tok", "wid"),
        P("tok", "wid"),
        P("wid", "tok"),
        P(),
        P(),
        P("tok"),
        P("tok", "wid", None),
        P("tok", "wid", None),
    )
    return jax.shard_map(
        shards,
        mesh=mesh,
        in_specs=placed,
        out_specs=(P("tok", "wid"), P("tok", "wid")),
        check_vma=False,
    )
```

```python
import functools

import jax
import jax.numpy as jnp
from jax import lax
from jax.experimental import pallas as pl
from jax.experimental.pallas import tpu as pltpu
from jax.sharding import PartitionSpec as P

HEADS = 20
KV_HEADS = 5
HEAD_DIM = 64
STRETCH = 512


EPSILON = 1e-05
MASKED = -1e30
SCORE_SCALE = 0.125


def norm_rows(values, gain):
    wide = values.astype(jnp.float32)
    mean_square = jnp.mean(wide * wide, axis=-1, keepdims=True)
    return (wide * lax.rsqrt(mean_square + EPSILON) * gain).astype(jnp.bfloat16)


def rotate(parts, places):
    half = parts.shape[-1] // 2
    ladder = jnp.arange(half).astype(jnp.float32) * (2.0 / parts.shape[-1])
    freqs = jnp.power(10000.0, -ladder)
    angles = places.astype(jnp.float32)[:, None] * freqs[None, :]
    cosine = jnp.cos(angles)[:, None, :]
    sine = jnp.sin(angles)[:, None, :]
    first = parts[..., :half]
    second = parts[..., half:]
    return jnp.concatenate(
        [first * cosine - second * sine, second * cosine + first * sine], axis=-1
    )


def shards_plain(hidden, w_qkv, w_out, w_gate, w_up, w_down, g_attn, g_ffn, lengths, k_cache, v_cache):
    wid_count = lax.axis_size("wid")
    wid_place = lax.axis_index("wid")
    row_count = hidden.shape[0]
    query_width = HEADS * HEAD_DIM
    kv_width = KV_HEADS * HEAD_DIM
    groups = HEADS // KV_HEADS
    full_rows = lax.all_gather(hidden, "wid", axis=1, tiled=True)
    normed = norm_rows(full_rows, g_attn)
    tall_cols = lax.all_gather(w_qkv, "tok", axis=0, tiled=True)
    own_cols = jnp.dot(normed, tall_cols, preferred_element_type=jnp.float32)
    mixed = lax.all_gather(own_cols.astype(jnp.bfloat16), "wid", axis=1, tiled=True)
    stretch_rows = lengths[0] + jnp.arange(STRETCH)
    places = jnp.concatenate([stretch_rows, lengths[1:]])
    query = rotate(
        mixed[:, :query_width].astype(jnp.float32).reshape(row_count, HEADS, HEAD_DIM), places
    ).astype(jnp.bfloat16)
    keys = rotate(
        mixed[:, query_width : query_width + kv_width]
        .astype(jnp.float32)
        .reshape(row_count, KV_HEADS, HEAD_DIM),
        places,
    ).astype(jnp.bfloat16)
    values = mixed[:, query_width + kv_width :]
    new_kv_all = jnp.concatenate([keys.reshape(row_count, kv_width), values], axis=1)
    kv_share = 2 * kv_width // wid_count
    new_kv = lax.dynamic_slice_in_dim(new_kv_all, wid_place * kv_share, kv_share, 1)
    value_heads = values.reshape(row_count, KV_HEADS, HEAD_DIM)
    span = k_cache.shape[1]
    requests = k_cache.shape[0]
    query_heads = query.reshape(row_count, KV_HEADS, groups, HEAD_DIM)
    old_keys = k_cache.reshape(requests, span, KV_HEADS, HEAD_DIM)
    old_values = v_cache.reshape(requests, span, KV_HEADS, HEAD_DIM)
    spots = wid_place * span + jnp.arange(span)
    live = spots[None, :] < lengths[:, None]
    score_stretch = (
        jnp.einsum(
            "rkgd,pkd->rkgp", query_heads[:STRETCH], old_keys[0], preferred_element_type=jnp.float32
        )
        * SCORE_SCALE
    )
    score_stretch = jnp.where(live[0][None, None, None, :], score_stretch, MASKED)
    score_decode = (
        jnp.einsum(
            "jkgd,jpkd->jkgp",
            query_heads[STRETCH:],
            old_keys[1:],
            preferred_element_type=jnp.float32,
        )
        * SCORE_SCALE
    )
    score_decode = jnp.where(live[1:][:, None, None, :], score_decode, MASKED)
    band = row_count // wid_count
    first_row = wid_place * band
    query_mine = lax.dynamic_slice_in_dim(query_heads, first_row, band, 0)
    later = first_row + jnp.arange(band)[:, None]
    earlier = jnp.arange(row_count)[None, :]
    fresh_ok = (later < STRETCH) & (earlier < STRETCH) & (earlier <= later) | (later >= STRETCH) & (
        earlier == later
    )
    score_fresh = (
        jnp.einsum("rkgd,jkd->rkgj", query_mine, keys, preferred_element_type=jnp.float32)
        * SCORE_SCALE
    )
    score_fresh = jnp.where(fresh_ok[:, None, None, :], score_fresh, MASKED)
    cache_peak = jnp.concatenate([score_stretch.max(-1), score_decode.max(-1)], axis=0)
    fresh_peak = lax.dynamic_update_slice_in_dim(
        jnp.full(cache_peak.shape, MASKED, jnp.float32), score_fresh.max(-1), first_row, 0
    )
    peak = lax.pmax(jnp.maximum(cache_peak, fresh_peak).astype(jnp.bfloat16), "wid").astype(
        jnp.float32
    )
    expo_stretch = jnp.exp(score_stretch - peak[:STRETCH, :, :, None])
    expo_decode = jnp.exp(score_decode - peak[STRETCH:, :, :, None])
    peak_mine = lax.dynamic_slice_in_dim(peak, first_row, band, 0)
    expo_fresh = jnp.exp(score_fresh - peak_mine[:, :, :, None])
    totals = jnp.concatenate([expo_stretch.sum(-1), expo_decode.sum(-1)], axis=0)
    sums = jnp.concatenate(
        [
            jnp.einsum(
                "rkgp,pkd->rkgd",
                expo_stretch.astype(jnp.bfloat16),
                old_values[0],
                preferred_element_type=jnp.float32,
            ),
            jnp.einsum(
                "jkgp,jpkd->jkgd",
                expo_decode.astype(jnp.bfloat16),
                old_values[1:],
                preferred_element_type=jnp.float32,
            ),
        ],
        axis=0,
    )
    fresh_sums = jnp.einsum(
        "rkgj,jkd->rkgd",
        expo_fresh.astype(jnp.bfloat16),
        value_heads,
        preferred_element_type=jnp.float32,
    )
    sums = lax.dynamic_update_slice_in_dim(
        sums, lax.dynamic_slice_in_dim(sums, first_row, band, 0) + fresh_sums, first_row, 0
    )
    totals = lax.dynamic_update_slice_in_dim(
        totals,
        lax.dynamic_slice_in_dim(totals, first_row, band, 0) + expo_fresh.sum(-1),
        first_row,
        0,
    )
    sums_all, totals_all = (
        lax.psum(sums.reshape(row_count, query_width).astype(jnp.bfloat16), "wid").astype(
            jnp.float32
        ),
        lax.psum(totals.reshape(row_count, HEADS).astype(jnp.bfloat16), "wid").astype(jnp.float32),
    )
    merged = sums_all.reshape(row_count, HEADS, HEAD_DIM) / totals_all[:, :, None]
    attended = merged.astype(jnp.bfloat16).reshape(row_count, query_width)
    out_whole = lax.all_gather(w_out, "tok", axis=0, tiled=True)
    projected = jnp.dot(attended, out_whole, preferred_element_type=jnp.float32)
    residual = hidden.astype(jnp.float32) + projected
    middle = residual.astype(jnp.bfloat16)
    middle_full = lax.all_gather(middle, "wid", axis=1, tiled=True)
    normed_ffn = norm_rows(middle_full, g_ffn)
    gate_whole, up_whole = (
        lax.all_gather(w_gate, "tok", axis=0, tiled=True),
        lax.all_gather(w_up, "tok", axis=0, tiled=True),
    )
    gate = jnp.dot(normed_ffn, gate_whole, preferred_element_type=jnp.float32)
    up = jnp.dot(normed_ffn, up_whole, preferred_element_type=jnp.float32)
    activated = (jax.nn.silu(gate) * up).astype(jnp.bfloat16)
    down_full = lax.all_gather(w_down, "tok", axis=1, tiled=True)
    own_sums = lax.psum_scatter(
        lax.dot_general(
            down_full, activated, (((0,), (1,)), ((), ())), preferred_element_type=jnp.float32
        ).astype(jnp.bfloat16),
        "wid",
        scatter_dimension=0,
        tiled=True,
    ).astype(jnp.float32)
    output = (residual + own_sums.T).astype(jnp.bfloat16)
    return (output, new_kv)


MESH = pl.DeviceIdType.MESH
CHUNKS = 3
VMEM_LIMIT = 56 * 1024 * 1024


def vmem():
    return pl.BlockSpec(memory_space=pltpu.VMEM)


def params(ident):
    return pltpu.CompilerParams(
        collective_id=ident, has_side_effects=True, vmem_limit_bytes=VMEM_LIMIT
    )


def greet(peers):
    barrier = pltpu.get_barrier_semaphore()
    for peer in peers:
        pl.semaphore_signal(barrier, inc=1, device_id=peer, device_id_type=MESH)
    pl.semaphore_wait(barrier, len(peers))


def push(src, dst, send, recv, peer):
    copy = pltpu.make_async_remote_copy(
        src_ref=src,
        dst_ref=dst,
        send_sem=send,
        recv_sem=recv,
        device_id=peer,
        device_id_type=MESH,
    )
    copy.start()
    return copy


def wid_peers(count):
    tok_place = lax.axis_index("tok")
    wid_place = lax.axis_index("wid")
    return [(tok_place, lax.rem(wid_place + k, count)) for k in range(1, count)]


def cuts(rows):
    size = rows // CHUNKS
    return [slice(c * size, (c + 1) * size) for c in range(CHUNKS)]


def share_rows(src, slots, at, send, recv, c, peers, place):
    return [
        push(src.at[at], slots.at[place, at], send.at[c, k], recv.at[c, k], peer)
        for k, peer in enumerate(peers)
    ]


def share(src, slots, send, recv, peers, place):
    return [push(src, slots.at[place], send.at[k], recv.at[k], peer) for k, peer in enumerate(peers)]


def tok_peers(toks):
    wid_place = lax.axis_index("wid")
    tok_place = lax.axis_index("tok")
    chips = toks // 2
    chip = tok_place // 2
    core = lax.rem(tok_place, 2)
    line = [(2 * lax.rem(chip + k, chips) + core, wid_place) for k in range(1, chips)]
    return line, (2 * chip + 1 - core, wid_place)


def fan(weight, slots, line, twin, send_b, recv_b, send_c, recv_c):
    tok_place = lax.axis_index("tok")
    line_copies = share(weight, slots, send_b, recv_b, line, tok_place)
    twin_copies = [push(weight, slots.at[tok_place], send_c.at[0], recv_c.at[0], twin)]
    slots[tok_place] = weight[...]
    return line_copies, twin_copies


def relay(slots, line_copies, twin_copies, toks, twin, send_c, recv_c):
    tok_place = lax.axis_index("tok")
    chips = toks // 2
    chip = tok_place // 2
    core = lax.rem(tok_place, 2)
    for k, copy in enumerate(line_copies):
        copy.wait_recv()
        slot = slots.at[2 * lax.rem(chip + chips - k - 1, chips) + core]
        twin_copies.append(push(slot, slot, send_c.at[k + 1], recv_c.at[k + 1], twin))


def mix_kernel(
    wids, toks, hidden, weight, gain, cosine, sine, turn, out,
    rows_all, weight_all, mixed_all, wide, send_a, recv_a, send_b, recv_b, send_c, recv_c, send_d, recv_d,
):
    wid_place = lax.axis_index("wid")
    peers = wid_peers(wids)
    line, twin = tok_peers(toks)
    greet(peers + line + [twin])
    line_copies, twin_copies = fan(weight, weight_all, line, twin, send_b, recv_b, send_c, recv_c)
    bands = cuts(hidden.shape[0])
    row_copies = [
        share_rows(hidden, rows_all, at, send_a, recv_a, c, peers, wid_place)
        for c, at in enumerate(bands)
    ]
    rows_all[wid_place] = hidden[...]
    relay(weight_all, line_copies, twin_copies, toks, twin, send_c, recv_c)
    for copy in twin_copies:
        copy.wait_recv()
    per = toks // wids
    width = weight.shape[1]
    mixed_copies = []
    for c, at in enumerate(bands):
        for copy in row_copies[c]:
            copy.wait_recv()
        square = 0.0
        for w in range(wids):
            part = rows_all[w, at].astype(jnp.float32)
            square = square + jnp.sum(part * part, axis=-1, keepdims=True)
        scale = lax.rsqrt(square * (1.0 / (wids * hidden.shape[1])) + EPSILON)
        total = 0.0
        for w in range(wids):
            normed = (rows_all[w, at].astype(jnp.float32) * scale * gain[w]).astype(jnp.bfloat16)
            block = weight_all[per * w : per * (w + 1)].reshape(hidden.shape[1], width)
            total = total + jnp.dot(normed, block, preferred_element_type=jnp.float32)
        mixed_all[wid_place, at] = total.astype(jnp.bfloat16)
        mixed_copies.append(
            share_rows(mixed_all.at[wid_place], mixed_all, at, send_d, recv_d, c, peers, wid_place)
        )
    turned = (HEADS + KV_HEADS) * HEAD_DIM
    for c, at in enumerate(bands):
        for copy in mixed_copies[c]:
            copy.wait_recv()
        for w in range(wids):
            wide[at, w * width : (w + 1) * width] = mixed_all[w, at].astype(jnp.float32)
        for start in range(0, wids * width, 128):
            part = wide[at, start : start + 128]
            if start < turned:
                swapped = jnp.dot(
                    part.astype(jnp.bfloat16), turn[...], preferred_element_type=jnp.float32
                )
                spun = part * cosine[at, :] + swapped * sine[at, :]
                if start + 128 > turned:
                    lane = lax.broadcasted_iota(jnp.int32, spun.shape, 1)
                    spun = jnp.where(lane < turned - start, spun, part)
                part = spun
            out[at, start : start + 128] = part.astype(jnp.bfloat16)
    for copy in sum(row_copies + mixed_copies, line_copies + twin_copies):
        copy.wait_send()


def mix(wids, toks, hidden, w_qkv, gain, cosine, sine, turn):
    rows, width = hidden.shape
    depth, columns = w_qkv.shape
    dma = pltpu.SemaphoreType.DMA
    chips = toks // 2
    return pl.pallas_call(
        functools.partial(mix_kernel, wids, toks),
        out_shape=jax.ShapeDtypeStruct((rows, wids * columns), jnp.bfloat16),
        in_specs=[vmem()] * 6,
        out_specs=vmem(),
        scratch_shapes=[
            pltpu.VMEM((wids, rows, width), jnp.bfloat16),
            pltpu.VMEM((toks, depth, columns), jnp.bfloat16),
            pltpu.VMEM((wids, rows, columns), jnp.bfloat16),
            pltpu.VMEM((rows, wids * columns), jnp.float32),
            dma((CHUNKS, wids - 1)), dma((CHUNKS, wids - 1)),
            dma((chips - 1,)), dma((chips - 1,)),
            dma((chips,)), dma((chips,)),
            dma((CHUNKS, wids - 1)), dma((CHUNKS, wids - 1)),
        ],
        compiler_params=params(0),
        cost_estimate=pl.CostEstimate(flops=10**10, bytes_accessed=10**8, transcendentals=0),
    )(hidden, w_qkv, gain, cosine, sine, turn)


def across(one, other):
    return lax.dot_general(
        one, other, (((1,), (1,)), ((), ())), preferred_element_type=jnp.float32
    )


def flip(values):
    return values.astype(jnp.float32).T.astype(jnp.bfloat16)


def partial_kernel(
    wids, lengths, mixed, spread, k_old, v_old, sums, stats, dec_sums, dec_stats, tall
):
    place = lax.axis_index("wid")
    span = k_old.shape[2]
    fresh = STRETCH // wids
    query_width = HEADS * HEAD_DIM
    kv_width = KV_HEADS * HEAD_DIM
    per = HEADS // wids
    groups = HEADS // KV_HEADS
    base = place * span
    first = pl.multiple_of(place * fresh, fresh)
    row = lax.broadcasted_iota(jnp.int32, (span + fresh, STRETCH), 1)
    spot = lax.broadcasted_iota(jnp.int32, (span + fresh, STRETCH), 0)
    limit = lengths[0] - base
    seen = ((spot < span) & (spot < limit)) | ((spot >= span) & (spot - span + first <= row))
    bias = jnp.where(seen, 0.0, MASKED)
    for g in range(KV_HEADS):
        at = g * HEAD_DIM
        held = query_width + kv_width + at
        new_keys = mixed[pl.ds(first, fresh), query_width + at : query_width + at + HEAD_DIM]
        new_values = mixed[pl.ds(first, fresh), held : held + HEAD_DIM]
        keys = jnp.concatenate([flip(k_old[0, at : at + HEAD_DIM, :]), new_keys], axis=0)
        values = jnp.concatenate([v_old[0, at : at + HEAD_DIM, :], flip(new_values)], axis=1)
        for h in range(g * groups, (g + 1) * groups):
            query = mixed[:STRETCH, h * HEAD_DIM : (h + 1) * HEAD_DIM] * jnp.bfloat16(SCORE_SCALE)
            score = across(keys, query) + bias
            peak = jnp.max(score, axis=0, keepdims=True)
            expo = jnp.exp(score - peak)
            total = jnp.sum(expo, axis=0, keepdims=True)
            tall[h * HEAD_DIM : (h + 1) * HEAD_DIM, :] = jnp.dot(
                values, expo.astype(jnp.bfloat16), preferred_element_type=jnp.float32
            )
            d, i = h // per, h % per
            stats[d, i : i + 1, :] = peak
            stats[d, 8 + i : 9 + i, :] = total
    for d in range(wids):
        sums[d] = tall[d * per * HEAD_DIM : (d + 1) * per * HEAD_DIM, :].T.astype(jnp.bfloat16)
        for i in range(per, 8):
            stats[d, i : i + 1, :] = jnp.ones((1, STRETCH), jnp.float32)
            stats[d, 8 + i : 9 + i, :] = jnp.ones((1, STRETCH), jnp.float32)
    rows = spread.shape[1]
    spots = lax.broadcasted_iota(jnp.int32, (rows, span), 1) + base

    def one(j, carry):
        query = spread[j]
        score = jnp.dot(query, k_old[j + 1], preferred_element_type=jnp.float32) * SCORE_SCALE
        score = jnp.where(spots < lengths[j + 1], score, MASKED)
        line = mixed[pl.ds(STRETCH, 16), query_width:].astype(jnp.float32)
        pick = lax.broadcasted_iota(jnp.int32, line.shape, 0) == j
        line = jnp.sum(jnp.where(pick, line, 0.0), axis=0, keepdims=True)
        own = (
            jnp.sum(query.astype(jnp.float32) * line[:, :kv_width], axis=1, keepdims=True)
            * SCORE_SCALE
        )
        own = jnp.where(place == 0, own, MASKED)
        peak = jnp.maximum(jnp.max(score, axis=1, keepdims=True), own)
        expo = jnp.exp(score - peak)
        expo_own = jnp.exp(own - peak)
        expo_own = jnp.where(place == 0, expo_own, 0.0)
        total = jnp.sum(expo, axis=1, keepdims=True) + expo_own
        part = across(expo.astype(jnp.bfloat16), v_old[j + 1])
        dec_sums[j] = part + expo_own * line[:, kv_width:]
        dec_stats[j, :, 0:1] = peak
        dec_stats[j, :, 1:2] = total
        return carry

    lax.fori_loop(0, k_old.shape[0] - 1, one, 0)


def partials(wids, lengths, mixed, spread, k_cache, v_cache):
    per = HEADS // wids
    count, rows, width = spread.shape
    return pl.pallas_call(
        functools.partial(partial_kernel, wids),
        out_shape=(
            jax.ShapeDtypeStruct((wids, STRETCH, per * HEAD_DIM), jnp.bfloat16),
            jax.ShapeDtypeStruct((wids, 16, STRETCH), jnp.float32),
            jax.ShapeDtypeStruct((count, rows, width), jnp.float32),
            jax.ShapeDtypeStruct((count, rows, 2), jnp.float32),
        ),
        in_specs=[pl.BlockSpec(memory_space=pltpu.SMEM)] + [vmem()] * 4,
        out_specs=(vmem(),) * 4,
        scratch_shapes=[pltpu.VMEM((HEADS * HEAD_DIM, STRETCH), jnp.float32)],
        compiler_params=pltpu.CompilerParams(vmem_limit_bytes=VMEM_LIMIT),
        cost_estimate=pl.CostEstimate(flops=10**10, bytes_accessed=10**8, transcendentals=10**7),
    )(lengths, mixed, spread, k_cache, v_cache)


def finish_kernel(
    wids, toks, sums, stats, hidden, w_out, w_down, w_gate, w_up, gain, spots, out,
    sums_all, stats_all, att_all, mid_all, part_all, part_own, residual, out_all, down_all, up_all,
    send_s, recv_s, send_p, recv_p, send_a, recv_a, send_m, recv_m, send_r, recv_r,
    send_b, recv_b, send_c, recv_c, send_d, recv_d, send_e, recv_e,
    send_u, recv_u, send_v, recv_v,
):
    place = lax.axis_index("wid")
    peers = wid_peers(wids)
    line, twin = tok_peers(toks)
    greet(peers + line + [twin])
    rows, width = hidden.shape
    bands = cuts(rows)
    stat_copies = [
        push(stats.at[peer[1]], stats_all.at[place], send_s.at[k], recv_s.at[k], peer)
        for k, peer in enumerate(peers)
    ]
    sum_copies = [
        [
            push(
                sums.at[peer[1], at], sums_all.at[place, at], send_p.at[c, k], recv_p.at[c, k], peer
            )
            for k, peer in enumerate(peers)
        ]
        for c, at in enumerate(bands)
    ]
    out_line, out_twin = fan(w_out, out_all, line, twin, send_b, recv_b, send_c, recv_c)
    up_line, up_twin = fan(w_up, up_all, line, twin, send_u, recv_u, send_v, recv_v)
    down_line, down_twin = fan(w_down, down_all, line, twin, send_d, recv_d, send_e, recv_e)
    stats_all[place] = stats[place]
    sums_all[place] = sums[place]
    for copy in stat_copies:
        copy.wait_recv()
    per = HEADS // wids
    peaks = [stats_all[w, :8, :] for w in range(wids)]
    totals = [stats_all[w, 8:, :] for w in range(wids)]
    peak = functools.reduce(jnp.maximum, peaks)
    factors = [jnp.exp(one - peak) for one in peaks]
    whole = functools.reduce(jnp.add, [f * t for f, t in zip(factors, totals)])
    shares = [
        lax.dot_general(
            f / whole, spots[...], (((0,), (0,)), ((), ())),
            precision=lax.Precision.HIGHEST, preferred_element_type=jnp.float32,
        )
        for f in factors
    ]
    att_copies = []
    for c, at in enumerate(bands):
        for copy in sum_copies[c]:
            copy.wait_recv()
        total = 0.0
        for w in range(wids):
            total = total + sums_all[w, at].astype(jnp.float32) * shares[w][at]
        att_all[place, at] = total.astype(jnp.bfloat16)
        att_copies.append(
            share_rows(att_all.at[place], att_all, at, send_a, recv_a, c, peers, place)
        )
    relay(out_all, out_line, out_twin, toks, twin, send_c, recv_c)
    for copy in out_twin:
        copy.wait_recv()
    ratio = toks // wids
    mid_copies = []
    for c, at in enumerate(bands):
        for copy in att_copies[c]:
            copy.wait_recv()
        total = hidden[at, :].astype(jnp.float32)
        for w in range(wids):
            block = out_all[ratio * w : ratio * (w + 1)].reshape(width, width)
            total = total + jnp.dot(att_all[w, at], block, preferred_element_type=jnp.float32)
        residual[at, :] = total
        mid_all[place, at] = total.astype(jnp.bfloat16)
        mid_copies.append(
            share_rows(mid_all.at[place], mid_all, at, send_m, recv_m, c, peers, place)
        )
    relay(up_all, up_line, up_twin, toks, twin, send_v, recv_v)
    relay(down_all, down_line, down_twin, toks, twin, send_e, recv_e)
    for copy in up_twin + down_twin:
        copy.wait_recv()
    part_copies = []
    for c, at in enumerate(bands):
        for copy in mid_copies[c]:
            copy.wait_recv()
        square = 0.0
        for w in range(wids):
            part = mid_all[w, at].astype(jnp.float32)
            square = square + jnp.sum(part * part, axis=-1, keepdims=True)
        scale = lax.rsqrt(square * (1.0 / (wids * width)) + EPSILON)
        gate = 0.0
        up = 0.0
        for w in range(wids):
            normed = (mid_all[w, at].astype(jnp.float32) * scale * gain[w]).astype(jnp.bfloat16)
            deep = slice(w * width, (w + 1) * width)
            gate = gate + jnp.dot(normed, w_gate[deep, :], preferred_element_type=jnp.float32)
            block = up_all[ratio * w : ratio * (w + 1)].reshape(width, w_up.shape[1])
            up = up + jnp.dot(normed, block, preferred_element_type=jnp.float32)
        active = (gate / (1.0 + jnp.exp(-gate)) * up).astype(jnp.bfloat16)
        sent = []
        for k in list(range(1, wids)) + [0]:
            dest = lax.rem(place + k, wids)
            block = down_all[pl.ds(dest * ratio, ratio)].reshape(width, w_down.shape[1])
            term = across(active, block)
            if k:
                part_own[k - 1, at] = term.astype(jnp.bfloat16)
                sent.append(
                    push(
                        part_own.at[k - 1, at], part_all.at[k - 1, at],
                        send_r.at[c, k - 1], recv_r.at[c, k - 1], peers[k - 1],
                    )
                )
            else:
                residual[at, :] = residual[at, :] + term
        part_copies.append(sent)
    for c, at in enumerate(bands):
        total = residual[at, :]
        for k, copy in enumerate(part_copies[c]):
            copy.wait_recv()
            total = total + part_all[k, at].astype(jnp.float32)
        out[at, :] = total.astype(jnp.bfloat16)
    singles = stat_copies + out_line + out_twin + up_line + up_twin + down_line + down_twin
    for copy in sum(sum_copies + att_copies + mid_copies + part_copies, singles):
        copy.wait_send()


def finish(wids, toks, sums, stats, hidden, w_out, w_down, w_gate, w_up, gain, spots):
    rows, width = hidden.shape
    dma = pltpu.SemaphoreType.DMA
    chips = toks // 2
    slots = pltpu.VMEM((wids, rows, width), jnp.bfloat16)
    fewer = pltpu.VMEM((wids - 1, rows, width), jnp.bfloat16)
    return pl.pallas_call(
        functools.partial(finish_kernel, wids, toks),
        out_shape=jax.ShapeDtypeStruct((rows, width), jnp.bfloat16),
        in_specs=[vmem()] * 9,
        out_specs=vmem(),
        scratch_shapes=[
            slots,
            pltpu.VMEM(stats.shape, jnp.float32),
            slots,
            slots,
            fewer,
            fewer,
            pltpu.VMEM((rows, width), jnp.float32),
            pltpu.VMEM((toks,) + w_out.shape, jnp.bfloat16),
            pltpu.VMEM((toks,) + w_down.shape, jnp.bfloat16),
            pltpu.VMEM((toks,) + w_up.shape, jnp.bfloat16),
        ]
        + [dma((wids - 1,))] * 2
        + [dma((CHUNKS, wids - 1))] * 8
        + [dma((chips - 1,)), dma((chips - 1,)), dma((chips,)), dma((chips,))] * 3,
        compiler_params=params(2),
        cost_estimate=pl.CostEstimate(flops=10**10, bytes_accessed=10**8, transcendentals=0),
    )(sums, stats, hidden, w_out, w_down, w_gate, w_up, gain, spots)


def shards_kernels(hidden, w_qkv, w_out, w_gate, w_up, w_down, g_attn, g_ffn, lengths, k_cache, v_cache):
    wids = lax.axis_size("wid")
    toks = lax.axis_size("tok")
    place = lax.axis_index("wid")
    rows, width = hidden.shape
    query_width = HEADS * HEAD_DIM
    kv_width = KV_HEADS * HEAD_DIM
    per = HEADS // wids
    groups = HEADS // KV_HEADS
    places = jnp.concatenate([lengths[0] + jnp.arange(STRETCH), lengths[1:]])
    half = HEAD_DIM // 2
    ladder = jnp.arange(half).astype(jnp.float32) * (2.0 / HEAD_DIM)
    freqs = jnp.power(10000.0, -ladder)
    angles = places.astype(jnp.float32)[:, None] * freqs[None, :]
    cos, sin = jnp.cos(angles), jnp.sin(angles)
    cosine = jnp.concatenate([cos, cos, cos, cos], axis=1)
    sine = jnp.concatenate([-sin, sin, -sin, sin], axis=1)
    lanes = jnp.arange(128)
    turn = (lanes[:, None] == (lanes ^ half)[None, :]).astype(jnp.bfloat16)
    mixed = mix(wids, toks, hidden, w_qkv, g_attn.reshape(wids, 1, width), cosine, sine, turn)
    w_gate, mixed = lax.optimization_barrier((w_gate, mixed))
    gate_whole = lax.all_gather(w_gate, "tok", axis=0, tiled=True)
    share_width = 2 * kv_width // wids
    new_kv = lax.dynamic_slice_in_dim(mixed, query_width + place * share_width, share_width, 1)
    count = rows - STRETCH
    own = mixed[STRETCH:, :query_width].reshape(count, HEADS, 1, HEAD_DIM)
    member = (jnp.arange(HEADS) // groups)[:, None] == jnp.arange(KV_HEADS)[None, :]
    spread = jnp.where(member[None, :, :, None], own, jnp.bfloat16(0)).reshape(count, HEADS, kv_width)
    spread = jnp.pad(spread, ((0, 0), (0, 32 - HEADS), (0, 0)))
    sums, stats, dec_sums, dec_stats = partials(
        wids, lengths, mixed, spread, k_cache.transpose(0, 2, 1), v_cache.transpose(0, 2, 1)
    )
    dec = dec_sums[:, :HEADS].reshape(count, HEADS, KV_HEADS, HEAD_DIM)
    dec = jnp.where(member[None, :, :, None], dec, 0.0).sum(2).astype(jnp.bfloat16)
    dec = dec.reshape(count, wids, per * HEAD_DIM).transpose(1, 0, 2)
    sums = jnp.concatenate([sums, dec], axis=1)
    dec_stats = dec_stats[:, :HEADS].reshape(count, wids, per, 2).transpose(1, 3, 2, 0)
    dec_stats = jnp.pad(
        dec_stats, ((0, 0), (0, 0), (0, 8 - per), (0, 0)), constant_values=1.0
    ).reshape(wids, 16, count)
    stats = jnp.concatenate([stats, dec_stats], axis=2)
    lanes_of = (jnp.arange(8)[:, None] == (jnp.arange(width) // HEAD_DIM)[None, :])
    output = finish(
        wids, toks, sums, stats, hidden, w_out, w_down.T, gate_whole,
        w_up, g_ffn.reshape(wids, 1, width), lanes_of.astype(jnp.float32),
    )
    return (output, new_kv)


def shards(*args):
    wids, toks = lax.axis_size("wid"), lax.axis_size("tok")
    fits = HEADS % wids == 0 and STRETCH % (128 * wids) == 0 and toks % (2 * wids) == 0
    fits = fits and args[0].shape[0] % (16 * CHUNKS) == 0 and args[1].shape[0] % 16 == 0 and HEADS // wids <= 8 and args[3].shape[1] % 128 == 0
    return (shards_kernels if fits else shards_plain)(*args)


def solution(mesh):
    placed = (
        P("tok", "wid"),
        P("tok", "wid"),
        P("tok", "wid"),
        P("tok", "wid"),
        P("tok", "wid"),
        P("wid", "tok"),
        P(),
        P(),
        P("tok"),
        P("tok", "wid", None),
        P("tok", "wid", None),
    )
    return jax.shard_map(
        shards,
        mesh=mesh,
        in_specs=placed,
        out_specs=(P("tok", "wid"), P("tok", "wid")),
        check_vma=False,
    )
```

```python
import functools

import jax
import jax.numpy as jnp
from jax import lax
from jax.experimental import pallas as pl
from jax.experimental.pallas import tpu as pltpu
from jax.sharding import PartitionSpec as P

HEADS = 20
KV_HEADS = 5
HEAD_DIM = 64
STRETCH = 512


EPSILON = 1e-05
MASKED = -1e30
SCORE_SCALE = 0.125


def norm_rows(values, gain):
    wide = values.astype(jnp.float32)
    mean_square = jnp.mean(wide * wide, axis=-1, keepdims=True)
    return (wide * lax.rsqrt(mean_square + EPSILON) * gain).astype(jnp.bfloat16)


def rotate(parts, places):
    half = parts.shape[-1] // 2
    ladder = jnp.arange(half).astype(jnp.float32) * (2.0 / parts.shape[-1])
    freqs = jnp.power(10000.0, -ladder)
    angles = places.astype(jnp.float32)[:, None] * freqs[None, :]
    cosine = jnp.cos(angles)[:, None, :]
    sine = jnp.sin(angles)[:, None, :]
    first = parts[..., :half]
    second = parts[..., half:]
    return jnp.concatenate(
        [first * cosine - second * sine, second * cosine + first * sine], axis=-1
    )


def shards_plain(hidden, w_qkv, w_out, w_gate, w_up, w_down, g_attn, g_ffn, lengths, k_cache, v_cache):
    wid_count = lax.axis_size("wid")
    wid_place = lax.axis_index("wid")
    row_count = hidden.shape[0]
    query_width = HEADS * HEAD_DIM
    kv_width = KV_HEADS * HEAD_DIM
    groups = HEADS // KV_HEADS
    full_rows = lax.all_gather(hidden, "wid", axis=1, tiled=True)
    normed = norm_rows(full_rows, g_attn)
    tall_cols = lax.all_gather(w_qkv, "tok", axis=0, tiled=True)
    own_cols = jnp.dot(normed, tall_cols, preferred_element_type=jnp.float32)
    mixed = lax.all_gather(own_cols.astype(jnp.bfloat16), "wid", axis=1, tiled=True)
    stretch_rows = lengths[0] + jnp.arange(STRETCH)
    places = jnp.concatenate([stretch_rows, lengths[1:]])
    query = rotate(
        mixed[:, :query_width].astype(jnp.float32).reshape(row_count, HEADS, HEAD_DIM), places
    ).astype(jnp.bfloat16)
    keys = rotate(
        mixed[:, query_width : query_width + kv_width]
        .astype(jnp.float32)
        .reshape(row_count, KV_HEADS, HEAD_DIM),
        places,
    ).astype(jnp.bfloat16)
    values = mixed[:, query_width + kv_width :]
    new_kv_all = jnp.concatenate([keys.reshape(row_count, kv_width), values], axis=1)
    kv_share = 2 * kv_width // wid_count
    new_kv = lax.dynamic_slice_in_dim(new_kv_all, wid_place * kv_share, kv_share, 1)
    value_heads = values.reshape(row_count, KV_HEADS, HEAD_DIM)
    span = k_cache.shape[1]
    requests = k_cache.shape[0]
    query_heads = query.reshape(row_count, KV_HEADS, groups, HEAD_DIM)
    old_keys = k_cache.reshape(requests, span, KV_HEADS, HEAD_DIM)
    old_values = v_cache.reshape(requests, span, KV_HEADS, HEAD_DIM)
    spots = wid_place * span + jnp.arange(span)
    live = spots[None, :] < lengths[:, None]
    score_stretch = (
        jnp.einsum(
            "rkgd,pkd->rkgp", query_heads[:STRETCH], old_keys[0], preferred_element_type=jnp.float32
        )
        * SCORE_SCALE
    )
    score_stretch = jnp.where(live[0][None, None, None, :], score_stretch, MASKED)
    score_decode = (
        jnp.einsum(
            "jkgd,jpkd->jkgp",
            query_heads[STRETCH:],
            old_keys[1:],
            preferred_element_type=jnp.float32,
        )
        * SCORE_SCALE
    )
    score_decode = jnp.where(live[1:][:, None, None, :], score_decode, MASKED)
    band = row_count // wid_count
    first_row = wid_place * band
    query_mine = lax.dynamic_slice_in_dim(query_heads, first_row, band, 0)
    later = first_row + jnp.arange(band)[:, None]
    earlier = jnp.arange(row_count)[None, :]
    fresh_ok = (later < STRETCH) & (earlier < STRETCH) & (earlier <= later) | (later >= STRETCH) & (
        earlier == later
    )
    score_fresh = (
        jnp.einsum("rkgd,jkd->rkgj", query_mine, keys, preferred_element_type=jnp.float32)
        * SCORE_SCALE
    )
    score_fresh = jnp.where(fresh_ok[:, None, None, :], score_fresh, MASKED)
    cache_peak = jnp.concatenate([score_stretch.max(-1), score_decode.max(-1)], axis=0)
    fresh_peak = lax.dynamic_update_slice_in_dim(
        jnp.full(cache_peak.shape, MASKED, jnp.float32), score_fresh.max(-1), first_row, 0
    )
    peak = lax.pmax(jnp.maximum(cache_peak, fresh_peak).astype(jnp.bfloat16), "wid").astype(
        jnp.float32
    )
    expo_stretch = jnp.exp(score_stretch - peak[:STRETCH, :, :, None])
    expo_decode = jnp.exp(score_decode - peak[STRETCH:, :, :, None])
    peak_mine = lax.dynamic_slice_in_dim(peak, first_row, band, 0)
    expo_fresh = jnp.exp(score_fresh - peak_mine[:, :, :, None])
    totals = jnp.concatenate([expo_stretch.sum(-1), expo_decode.sum(-1)], axis=0)
    sums = jnp.concatenate(
        [
            jnp.einsum(
                "rkgp,pkd->rkgd",
                expo_stretch.astype(jnp.bfloat16),
                old_values[0],
                preferred_element_type=jnp.float32,
            ),
            jnp.einsum(
                "jkgp,jpkd->jkgd",
                expo_decode.astype(jnp.bfloat16),
                old_values[1:],
                preferred_element_type=jnp.float32,
            ),
        ],
        axis=0,
    )
    fresh_sums = jnp.einsum(
        "rkgj,jkd->rkgd",
        expo_fresh.astype(jnp.bfloat16),
        value_heads,
        preferred_element_type=jnp.float32,
    )
    sums = lax.dynamic_update_slice_in_dim(
        sums, lax.dynamic_slice_in_dim(sums, first_row, band, 0) + fresh_sums, first_row, 0
    )
    totals = lax.dynamic_update_slice_in_dim(
        totals,
        lax.dynamic_slice_in_dim(totals, first_row, band, 0) + expo_fresh.sum(-1),
        first_row,
        0,
    )
    sums_all, totals_all = (
        lax.psum(sums.reshape(row_count, query_width).astype(jnp.bfloat16), "wid").astype(
            jnp.float32
        ),
        lax.psum(totals.reshape(row_count, HEADS).astype(jnp.bfloat16), "wid").astype(jnp.float32),
    )
    merged = sums_all.reshape(row_count, HEADS, HEAD_DIM) / totals_all[:, :, None]
    attended = merged.astype(jnp.bfloat16).reshape(row_count, query_width)
    out_whole = lax.all_gather(w_out, "tok", axis=0, tiled=True)
    projected = jnp.dot(attended, out_whole, preferred_element_type=jnp.float32)
    residual = hidden.astype(jnp.float32) + projected
    middle = residual.astype(jnp.bfloat16)
    middle_full = lax.all_gather(middle, "wid", axis=1, tiled=True)
    normed_ffn = norm_rows(middle_full, g_ffn)
    gate_whole, up_whole = (
        lax.all_gather(w_gate, "tok", axis=0, tiled=True),
        lax.all_gather(w_up, "tok", axis=0, tiled=True),
    )
    gate = jnp.dot(normed_ffn, gate_whole, preferred_element_type=jnp.float32)
    up = jnp.dot(normed_ffn, up_whole, preferred_element_type=jnp.float32)
    activated = (jax.nn.silu(gate) * up).astype(jnp.bfloat16)
    down_full = lax.all_gather(w_down, "tok", axis=1, tiled=True)
    own_sums = lax.psum_scatter(
        lax.dot_general(
            down_full, activated, (((0,), (1,)), ((), ())), preferred_element_type=jnp.float32
        ).astype(jnp.bfloat16),
        "wid",
        scatter_dimension=0,
        tiled=True,
    ).astype(jnp.float32)
    output = (residual + own_sums.T).astype(jnp.bfloat16)
    return (output, new_kv)


MESH = pl.DeviceIdType.MESH
CHUNKS = 3
VMEM_LIMIT = 56 * 1024 * 1024


def vmem():
    return pl.BlockSpec(memory_space=pltpu.VMEM)


def params(ident):
    return pltpu.CompilerParams(
        collective_id=ident, has_side_effects=True, vmem_limit_bytes=VMEM_LIMIT
    )


def greet(peers):
    barrier = pltpu.get_barrier_semaphore()
    for peer in peers:
        pl.semaphore_signal(barrier, inc=1, device_id=peer, device_id_type=MESH)
    pl.semaphore_wait(barrier, len(peers))


def push(src, dst, send, recv, peer):
    copy = pltpu.make_async_remote_copy(
        src_ref=src,
        dst_ref=dst,
        send_sem=send,
        recv_sem=recv,
        device_id=peer,
        device_id_type=MESH,
    )
    copy.start()
    return copy


def wid_peers(count):
    tok_place = lax.axis_index("tok")
    wid_place = lax.axis_index("wid")
    return [(tok_place, lax.rem(wid_place + k, count)) for k in range(1, count)]


def cuts(rows):
    size = rows // CHUNKS
    return [slice(c * size, (c + 1) * size) for c in range(CHUNKS)]


def share_rows(src, slots, at, send, recv, c, peers, place):
    return [
        push(src.at[at], slots.at[place, at], send.at[c, k], recv.at[c, k], peer)
        for k, peer in enumerate(peers)
    ]


def share(src, slots, send, recv, peers, place):
    return [push(src, slots.at[place], send.at[k], recv.at[k], peer) for k, peer in enumerate(peers)]


def tok_peers(toks):
    wid_place = lax.axis_index("wid")
    tok_place = lax.axis_index("tok")
    chips = toks // 2
    chip = tok_place // 2
    core = lax.rem(tok_place, 2)
    line = [(2 * lax.rem(chip + k, chips) + core, wid_place) for k in range(1, chips)]
    return line, (2 * chip + 1 - core, wid_place)


def fan(weight, slots, line, twin, send_b, recv_b, send_c, recv_c):
    tok_place = lax.axis_index("tok")
    line_copies = share(weight, slots, send_b, recv_b, line, tok_place)
    twin_copies = [push(weight, slots.at[tok_place], send_c.at[0], recv_c.at[0], twin)]
    slots[tok_place] = weight[...]
    return line_copies, twin_copies


def relay(slots, line_copies, twin_copies, toks, twin, send_c, recv_c):
    tok_place = lax.axis_index("tok")
    chips = toks // 2
    chip = tok_place // 2
    core = lax.rem(tok_place, 2)
    for k, copy in enumerate(line_copies):
        copy.wait_recv()
        slot = slots.at[2 * lax.rem(chip + chips - k - 1, chips) + core]
        twin_copies.append(push(slot, slot, send_c.at[k + 1], recv_c.at[k + 1], twin))


def mix_kernel(
    wids, toks, hidden, weight, gain, cosine, sine, turn, out,
    rows_all, weight_all, mixed_all, wide, send_a, recv_a, send_b, recv_b, send_c, recv_c, send_d, recv_d,
):
    wid_place = lax.axis_index("wid")
    peers = wid_peers(wids)
    line, twin = tok_peers(toks)
    greet(peers + line + [twin])
    line_copies, twin_copies = fan(weight, weight_all, line, twin, send_b, recv_b, send_c, recv_c)
    bands = cuts(hidden.shape[0])
    row_copies = [
        share_rows(hidden, rows_all, at, send_a, recv_a, c, peers, wid_place)
        for c, at in enumerate(bands)
    ]
    rows_all[wid_place] = hidden[...]
    relay(weight_all, line_copies, twin_copies, toks, twin, send_c, recv_c)
    for copy in twin_copies:
        copy.wait_recv()
    per = toks // wids
    width = weight.shape[1]
    mixed_copies = []
    for c, at in enumerate(bands):
        for copy in row_copies[c]:
            copy.wait_recv()
        square = 0.0
        for w in range(wids):
            part = rows_all[w, at].astype(jnp.float32)
            square = square + jnp.sum(part * part, axis=-1, keepdims=True)
        scale = lax.rsqrt(square * (1.0 / (wids * hidden.shape[1])) + EPSILON)
        total = 0.0
        for w in range(wids):
            normed = (rows_all[w, at].astype(jnp.float32) * scale * gain[w]).astype(jnp.bfloat16)
            block = weight_all[per * w : per * (w + 1)].reshape(hidden.shape[1], width)
            total = total + jnp.dot(normed, block, preferred_element_type=jnp.float32)
        mixed_all[wid_place, at] = total.astype(jnp.bfloat16)
        mixed_copies.append(
            share_rows(mixed_all.at[wid_place], mixed_all, at, send_d, recv_d, c, peers, wid_place)
        )
    turned = (HEADS + KV_HEADS) * HEAD_DIM
    for c, at in enumerate(bands):
        for copy in mixed_copies[c]:
            copy.wait_recv()
        for w in range(wids):
            wide[at, w * width : (w + 1) * width] = mixed_all[w, at].astype(jnp.float32)
        for start in range(0, wids * width, 128):
            part = wide[at, start : start + 128]
            if start < turned:
                swapped = jnp.dot(
                    part.astype(jnp.bfloat16), turn[...], preferred_element_type=jnp.float32
                )
                spun = part * cosine[at, :] + swapped * sine[at, :]
                if start + 128 > turned:
                    lane = lax.broadcasted_iota(jnp.int32, spun.shape, 1)
                    spun = jnp.where(lane < turned - start, spun, part)
                part = spun
            out[at, start : start + 128] = part.astype(jnp.bfloat16)
    for copy in sum(row_copies + mixed_copies, line_copies + twin_copies):
        copy.wait_send()


def mix(wids, toks, hidden, w_qkv, gain, cosine, sine, turn):
    rows, width = hidden.shape
    depth, columns = w_qkv.shape
    dma = pltpu.SemaphoreType.DMA
    chips = toks // 2
    return pl.pallas_call(
        functools.partial(mix_kernel, wids, toks),
        out_shape=jax.ShapeDtypeStruct((rows, wids * columns), jnp.bfloat16),
        in_specs=[vmem()] * 6,
        out_specs=vmem(),
        scratch_shapes=[
            pltpu.VMEM((wids, rows, width), jnp.bfloat16),
            pltpu.VMEM((toks, depth, columns), jnp.bfloat16),
            pltpu.VMEM((wids, rows, columns), jnp.bfloat16),
            pltpu.VMEM((rows, wids * columns), jnp.float32),
            dma((CHUNKS, wids - 1)), dma((CHUNKS, wids - 1)),
            dma((chips - 1,)), dma((chips - 1,)),
            dma((chips,)), dma((chips,)),
            dma((CHUNKS, wids - 1)), dma((CHUNKS, wids - 1)),
        ],
        compiler_params=params(0),
        cost_estimate=pl.CostEstimate(flops=10**10, bytes_accessed=10**8, transcendentals=0),
    )(hidden, w_qkv, gain, cosine, sine, turn)


def across(one, other):
    return lax.dot_general(
        one, other, (((1,), (1,)), ((), ())), preferred_element_type=jnp.float32
    )


def flip(values):
    return values.astype(jnp.float32).T.astype(jnp.bfloat16)


def partial_kernel(
    wids, lengths, mixed, spread, k_old, v_old, sums, stats, dec_sums, dec_stats, tall
):
    place = lax.axis_index("wid")
    span = k_old.shape[2]
    fresh = STRETCH // wids
    query_width = HEADS * HEAD_DIM
    kv_width = KV_HEADS * HEAD_DIM
    per = HEADS // wids
    groups = HEADS // KV_HEADS
    base = place * span
    first = pl.multiple_of(place * fresh, fresh)
    row = lax.broadcasted_iota(jnp.int32, (span + fresh, STRETCH), 1)
    spot = lax.broadcasted_iota(jnp.int32, (span + fresh, STRETCH), 0)
    limit = lengths[0] - base
    seen = ((spot < span) & (spot < limit)) | ((spot >= span) & (spot - span + first <= row))
    bias = jnp.where(seen, 0.0, MASKED)
    for g in range(KV_HEADS):
        at = g * HEAD_DIM
        held = query_width + kv_width + at
        new_keys = mixed[pl.ds(first, fresh), query_width + at : query_width + at + HEAD_DIM]
        new_values = mixed[pl.ds(first, fresh), held : held + HEAD_DIM]
        keys = jnp.concatenate([flip(k_old[0, at : at + HEAD_DIM, :]), new_keys], axis=0)
        values = jnp.concatenate([v_old[0, at : at + HEAD_DIM, :], flip(new_values)], axis=1)
        for h in range(g * groups, (g + 1) * groups):
            query = mixed[:STRETCH, h * HEAD_DIM : (h + 1) * HEAD_DIM] * jnp.bfloat16(SCORE_SCALE)
            score = across(keys, query) + bias
            peak = jnp.max(score, axis=0, keepdims=True)
            expo = jnp.exp(score - peak)
            total = jnp.sum(expo, axis=0, keepdims=True)
            tall[h * HEAD_DIM : (h + 1) * HEAD_DIM, :] = jnp.dot(
                values, expo.astype(jnp.bfloat16), preferred_element_type=jnp.float32
            )
            d, i = h // per, h % per
            stats[d, i : i + 1, :] = peak
            stats[d, 8 + i : 9 + i, :] = total
    for d in range(wids):
        sums[d] = tall[d * per * HEAD_DIM : (d + 1) * per * HEAD_DIM, :].T.astype(jnp.bfloat16)
        for i in range(per, 8):
            stats[d, i : i + 1, :] = jnp.ones((1, STRETCH), jnp.float32)
            stats[d, 8 + i : 9 + i, :] = jnp.ones((1, STRETCH), jnp.float32)
    rows = spread.shape[1]
    spots = lax.broadcasted_iota(jnp.int32, (rows, span), 1) + base

    tail = mixed[STRETCH:, query_width:].astype(jnp.float32)
    for j in range(k_old.shape[0] - 1):
        query = spread[j]
        score = jnp.dot(query, k_old[j + 1], preferred_element_type=jnp.float32) * SCORE_SCALE
        score = jnp.where(spots < lengths[j + 1], score, MASKED)
        line = tail[j : j + 1]
        own = (
            jnp.sum(query.astype(jnp.float32) * line[:, :kv_width], axis=1, keepdims=True)
            * SCORE_SCALE
        )
        own = jnp.where(place == 0, own, MASKED)
        peak = jnp.maximum(jnp.max(score, axis=1, keepdims=True), own)
        expo = jnp.exp(score - peak)
        expo_own = jnp.exp(own - peak)
        expo_own = jnp.where(place == 0, expo_own, 0.0)
        total = jnp.sum(expo, axis=1, keepdims=True) + expo_own
        part = across(expo.astype(jnp.bfloat16), v_old[j + 1])
        dec_sums[j] = part + expo_own * line[:, kv_width:]
        dec_stats[j, :, 0:1] = peak
        dec_stats[j, :, 1:2] = total


def partials(wids, lengths, mixed, spread, k_cache, v_cache):
    per = HEADS // wids
    count, rows, width = spread.shape
    return pl.pallas_call(
        functools.partial(partial_kernel, wids),
        out_shape=(
            jax.ShapeDtypeStruct((wids, STRETCH, per * HEAD_DIM), jnp.bfloat16),
            jax.ShapeDtypeStruct((wids, 16, STRETCH), jnp.float32),
            jax.ShapeDtypeStruct((count, rows, width), jnp.float32),
            jax.ShapeDtypeStruct((count, rows, 2), jnp.float32),
        ),
        in_specs=[pl.BlockSpec(memory_space=pltpu.SMEM)] + [vmem()] * 4,
        out_specs=(vmem(),) * 4,
        scratch_shapes=[pltpu.VMEM((HEADS * HEAD_DIM, STRETCH), jnp.float32)],
        compiler_params=pltpu.CompilerParams(vmem_limit_bytes=VMEM_LIMIT),
        cost_estimate=pl.CostEstimate(flops=10**10, bytes_accessed=10**8, transcendentals=10**7),
    )(lengths, mixed, spread, k_cache, v_cache)


def finish_kernel(
    wids, toks, sums, stats, hidden, w_out, w_down, w_gate, w_up, gain, spots, out,
    sums_all, stats_all, att_all, mid_all, part_all, part_own, residual, out_all, down_all, up_all,
    send_s, recv_s, send_p, recv_p, send_a, recv_a, send_m, recv_m, send_r, recv_r,
    send_b, recv_b, send_c, recv_c, send_d, recv_d, send_e, recv_e,
    send_u, recv_u, send_v, recv_v,
):
    place = lax.axis_index("wid")
    peers = wid_peers(wids)
    line, twin = tok_peers(toks)
    greet(peers + line + [twin])
    rows, width = hidden.shape
    bands = cuts(rows)
    stat_copies = [
        push(stats.at[peer[1]], stats_all.at[place], send_s.at[k], recv_s.at[k], peer)
        for k, peer in enumerate(peers)
    ]
    sum_copies = [
        [
            push(
                sums.at[peer[1], at], sums_all.at[place, at], send_p.at[c, k], recv_p.at[c, k], peer
            )
            for k, peer in enumerate(peers)
        ]
        for c, at in enumerate(bands)
    ]
    out_line, out_twin = fan(w_out, out_all, line, twin, send_b, recv_b, send_c, recv_c)
    up_line, up_twin = fan(w_up, up_all, line, twin, send_u, recv_u, send_v, recv_v)
    down_line, down_twin = fan(w_down, down_all, line, twin, send_d, recv_d, send_e, recv_e)
    stats_all[place] = stats[place]
    sums_all[place] = sums[place]
    for copy in stat_copies:
        copy.wait_recv()
    per = HEADS // wids
    peaks = [stats_all[w, :8, :] for w in range(wids)]
    totals = [stats_all[w, 8:, :] for w in range(wids)]
    peak = functools.reduce(jnp.maximum, peaks)
    factors = [jnp.exp(one - peak) for one in peaks]
    whole = functools.reduce(jnp.add, [f * t for f, t in zip(factors, totals)])
    shares = [
        lax.dot_general(
            f / whole, spots[...], (((0,), (0,)), ((), ())),
            precision=lax.Precision.HIGHEST, preferred_element_type=jnp.float32,
        )
        for f in factors
    ]
    att_copies = []
    for c, at in enumerate(bands):
        for copy in sum_copies[c]:
            copy.wait_recv()
        total = 0.0
        for w in range(wids):
            total = total + sums_all[w, at].astype(jnp.float32) * shares[w][at]
        att_all[place, at] = total.astype(jnp.bfloat16)
        att_copies.append(
            share_rows(att_all.at[place], att_all, at, send_a, recv_a, c, peers, place)
        )
    relay(out_all, out_line, out_twin, toks, twin, send_c, recv_c)
    for copy in out_twin:
        copy.wait_recv()
    ratio = toks // wids
    mid_copies = []
    for c, at in enumerate(bands):
        for copy in att_copies[c]:
            copy.wait_recv()
        total = hidden[at, :].astype(jnp.float32)
        for w in range(wids):
            block = out_all[ratio * w : ratio * (w + 1)].reshape(width, width)
            total = total + jnp.dot(att_all[w, at], block, preferred_element_type=jnp.float32)
        residual[at, :] = total
        mid_all[place, at] = total.astype(jnp.bfloat16)
        mid_copies.append(
            share_rows(mid_all.at[place], mid_all, at, send_m, recv_m, c, peers, place)
        )
    relay(up_all, up_line, up_twin, toks, twin, send_v, recv_v)
    relay(down_all, down_line, down_twin, toks, twin, send_e, recv_e)
    for copy in up_twin + down_twin:
        copy.wait_recv()
    part_copies = []
    for c, at in enumerate(bands):
        for copy in mid_copies[c]:
            copy.wait_recv()
        square = 0.0
        for w in range(wids):
            part = mid_all[w, at].astype(jnp.float32)
            square = square + jnp.sum(part * part, axis=-1, keepdims=True)
        scale = lax.rsqrt(square * (1.0 / (wids * width)) + EPSILON)
        gate = 0.0
        up = 0.0
        for w in range(wids):
            normed = (mid_all[w, at].astype(jnp.float32) * scale * gain[w]).astype(jnp.bfloat16)
            deep = slice(w * width, (w + 1) * width)
            gate = gate + jnp.dot(normed, w_gate[deep, :], preferred_element_type=jnp.float32)
            block = up_all[ratio * w : ratio * (w + 1)].reshape(width, w_up.shape[1])
            up = up + jnp.dot(normed, block, preferred_element_type=jnp.float32)
        active = (gate / (1.0 + jnp.exp(-gate)) * up).astype(jnp.bfloat16)
        sent = []
        for k in list(range(1, wids)) + [0]:
            dest = lax.rem(place + k, wids)
            block = down_all[pl.ds(dest * ratio, ratio)].reshape(width, w_down.shape[1])
            term = across(active, block)
            if k:
                part_own[k - 1, at] = term.astype(jnp.bfloat16)
                sent.append(
                    push(
                        part_own.at[k - 1, at], part_all.at[k - 1, at],
                        send_r.at[c, k - 1], recv_r.at[c, k - 1], peers[k - 1],
                    )
                )
            else:
                residual[at, :] = residual[at, :] + term
        part_copies.append(sent)
    for c, at in enumerate(bands):
        total = residual[at, :]
        for k, copy in enumerate(part_copies[c]):
            copy.wait_recv()
            total = total + part_all[k, at].astype(jnp.float32)
        out[at, :] = total.astype(jnp.bfloat16)
    singles = stat_copies + out_line + out_twin + up_line + up_twin + down_line + down_twin
    for copy in sum(sum_copies + att_copies + mid_copies + part_copies, singles):
        copy.wait_send()


def finish(wids, toks, sums, stats, hidden, w_out, w_down, w_gate, w_up, gain, spots):
    rows, width = hidden.shape
    dma = pltpu.SemaphoreType.DMA
    chips = toks // 2
    slots = pltpu.VMEM((wids, rows, width), jnp.bfloat16)
    fewer = pltpu.VMEM((wids - 1, rows, width), jnp.bfloat16)
    return pl.pallas_call(
        functools.partial(finish_kernel, wids, toks),
        out_shape=jax.ShapeDtypeStruct((rows, width), jnp.bfloat16),
        in_specs=[vmem()] * 9,
        out_specs=vmem(),
        scratch_shapes=[
            slots,
            pltpu.VMEM(stats.shape, jnp.float32),
            slots,
            slots,
            fewer,
            fewer,
            pltpu.VMEM((rows, width), jnp.float32),
            pltpu.VMEM((toks,) + w_out.shape, jnp.bfloat16),
            pltpu.VMEM((toks,) + w_down.shape, jnp.bfloat16),
            pltpu.VMEM((toks,) + w_up.shape, jnp.bfloat16),
        ]
        + [dma((wids - 1,))] * 2
        + [dma((CHUNKS, wids - 1))] * 8
        + [dma((chips - 1,)), dma((chips - 1,)), dma((chips,)), dma((chips,))] * 3,
        compiler_params=params(2),
        cost_estimate=pl.CostEstimate(flops=10**10, bytes_accessed=10**8, transcendentals=0),
    )(sums, stats, hidden, w_out, w_down, w_gate, w_up, gain, spots)


def shards_kernels(hidden, w_qkv, w_out, w_gate, w_up, w_down, g_attn, g_ffn, lengths, k_cache, v_cache):
    wids = lax.axis_size("wid")
    toks = lax.axis_size("tok")
    place = lax.axis_index("wid")
    rows, width = hidden.shape
    query_width = HEADS * HEAD_DIM
    kv_width = KV_HEADS * HEAD_DIM
    per = HEADS // wids
    groups = HEADS // KV_HEADS
    places = jnp.concatenate([lengths[0] + jnp.arange(STRETCH), lengths[1:]])
    half = HEAD_DIM // 2
    ladder = jnp.arange(half).astype(jnp.float32) * (2.0 / HEAD_DIM)
    freqs = jnp.power(10000.0, -ladder)
    angles = places.astype(jnp.float32)[:, None] * freqs[None, :]
    cos, sin = jnp.cos(angles), jnp.sin(angles)
    cosine = jnp.concatenate([cos, cos, cos, cos], axis=1)
    sine = jnp.concatenate([-sin, sin, -sin, sin], axis=1)
    lanes = jnp.arange(128)
    turn = (lanes[:, None] == (lanes ^ half)[None, :]).astype(jnp.bfloat16)
    mixed = mix(wids, toks, hidden, w_qkv, g_attn.reshape(wids, 1, width), cosine, sine, turn)
    w_gate, mixed = lax.optimization_barrier((w_gate, mixed))
    gate_whole = lax.all_gather(w_gate, "tok", axis=0, tiled=True)
    share_width = 2 * kv_width // wids
    new_kv = lax.dynamic_slice_in_dim(mixed, query_width + place * share_width, share_width, 1)
    count = rows - STRETCH
    own = mixed[STRETCH:, :query_width].reshape(count, HEADS, 1, HEAD_DIM)
    member = (jnp.arange(HEADS) // groups)[:, None] == jnp.arange(KV_HEADS)[None, :]
    spread = jnp.where(member[None, :, :, None], own, jnp.bfloat16(0)).reshape(count, HEADS, kv_width)
    spread = jnp.pad(spread, ((0, 0), (0, 32 - HEADS), (0, 0)))
    sums, stats, dec_sums, dec_stats = partials(
        wids, lengths, mixed, spread, k_cache.transpose(0, 2, 1), v_cache.transpose(0, 2, 1)
    )
    dec = dec_sums[:, :HEADS].reshape(count, HEADS, KV_HEADS, HEAD_DIM)
    dec = jnp.where(member[None, :, :, None], dec, 0.0).sum(2).astype(jnp.bfloat16)
    dec = dec.reshape(count, wids, per * HEAD_DIM).transpose(1, 0, 2)
    sums = jnp.concatenate([sums, dec], axis=1)
    dec_stats = dec_stats[:, :HEADS].reshape(count, wids, per, 2).transpose(1, 3, 2, 0)
    dec_stats = jnp.pad(
        dec_stats, ((0, 0), (0, 0), (0, 8 - per), (0, 0)), constant_values=1.0
    ).reshape(wids, 16, count)
    stats = jnp.concatenate([stats, dec_stats], axis=2)
    lanes_of = (jnp.arange(8)[:, None] == (jnp.arange(width) // HEAD_DIM)[None, :])
    output = finish(
        wids, toks, sums, stats, hidden, w_out, w_down.T, gate_whole,
        w_up, g_ffn.reshape(wids, 1, width), lanes_of.astype(jnp.float32),
    )
    return (output, new_kv)


def shards(*args):
    wids, toks = lax.axis_size("wid"), lax.axis_size("tok")
    fits = HEADS % wids == 0 and STRETCH % (128 * wids) == 0 and toks % (2 * wids) == 0
    fits = fits and args[0].shape[0] % (16 * CHUNKS) == 0 and args[1].shape[0] % 16 == 0 and HEADS // wids <= 8 and args[3].shape[1] % 128 == 0
    return (shards_kernels if fits else shards_plain)(*args)


def solution(mesh):
    placed = (
        P("tok", "wid"),
        P("tok", "wid"),
        P("tok", "wid"),
        P("tok", "wid"),
        P("tok", "wid"),
        P("wid", "tok"),
        P(),
        P(),
        P("tok"),
        P("tok", "wid", None),
        P("tok", "wid", None),
    )
    return jax.shard_map(
        shards,
        mesh=mesh,
        in_specs=placed,
        out_specs=(P("tok", "wid"), P("tok", "wid")),
        check_vma=False,
    )
```
